128 devices in a mesh: var: 8 (over z, x_hi), patch: 8 (over y, core), win: 2 (over x_lo).
Axes of the slice: x: 4 (x_hi: 2, x_lo: 2; x = x_hi * 2 + x_lo), y: 4, z: 4, core: 2. Of those that a mesh axis runs over, the one named last changes fastest.
Arguments:
- fields: bfloat16 [480, 16, 1024], P(('win', 'var'), 'patch'), parts along dimension 0, may hold values from -6 to 6
- var_ids: int32 [240], replicated, may hold values from 0 to 239, each once
- level_of: int32 [240], replicated, may hold values from 0 to 37
- window_offset: int32 [2], P('win'), parts along dimension 0, may hold values from 0 to 164
- w_embed: bfloat16 [240, 16, 512], replicated, may hold values from -1.5 to 1.5
- var_emb: bfloat16 [240, 512], replicated, may hold values from -6 to 6
- w_key: bfloat16 [512, 512], replicated, may hold values from -0.25 to 0.25
- w_value: bfloat16 [512, 512], replicated, may hold values from -0.25 to 0.25
- w_out: bfloat16 [512, 512], replicated, may hold values from -0.25 to 0.25
- latent_query: float32 [8, 64], replicated, may hold values from -9 to 9
- bias_table: float32 [38, 8], replicated, may hold values from -4 to 300
- lat_emb: bfloat16 [180, 512], replicated, may hold values from -3 to 3
- d_aggregated: bfloat16 [32, 64, 512], P('win', ('var', 'patch')), parts along dimension 0, may hold values from -6 to 6
Outputs:
- aggregated: bfloat16 [32, 64, 512], P('win', ('var', 'patch')), parts along dimension 0
- embed_grad_rows: float32 [480, 16, 512], P(('win', 'var')), parts along dimension 0
- var_grad_rows: float32 [480, 512], P(('win', 'var')), parts along dimension 0
- key_grad: float32 [1024, 512], P('win'), parts along dimension 0
- value_grad: float32 [1024, 512], P('win'), parts along dimension 0
The draws below stay inside these ranges and needn't reach their ends.
There are 2 independent parts, one for each index of `win`. The reference program is written for one: setup_inputs(seed, part) draws one part's arguments, and reference() takes and returns one part's arrays. A program takes and returns all parts, laid end to end along the dimension named above; an argument that names none is the same for every part. Nothing has to cross between parts.
All inputs are finite; a program needn't handle non-finite values.
Results may differ from the reference program's by a relative error of at most 0.017.
Values may be sent and summed in bfloat16 or wider, within the bound.
A program may use at most 128 MiB of HBM per device.

```python
import jax
import jax.numpy as jnp
from jax import lax

V = 240
PIX = 16
D = 512
H = 8
DH = 64
NLEV = 38
LAT = 180
ROWS = 16
COLS = 64


def draw_bias_table(key, part):
    key = jax.random.fold_in(key, 11)
    second_key = jax.random.fold_in(key, 1)
    return jnp.clip(jax.random.normal(second_key, (NLEV, H), jnp.float32), -4.0, 4.0)


def place_ends(values, stream_key, low, top_value):
    place = [jax.random.randint(jax.random.fold_in(stream_key, axis), (), 0, length) for axis, length in enumerate(values.shape)]
    longest = values.shape.index(max(values.shape))
    beside = place[:longest] + [(place[longest] + 1) % values.shape[longest]] + place[longest + 1:]
    return values.at[tuple(place)].set(low).at[tuple(beside)].set(top_value)


def block_scale(own_key, dims, pieces, low, high):
    factor_of = 1.0
    for dim, parts in pieces:
        draws = jax.random.uniform(jax.random.fold_in(jax.random.fold_in(own_key, 6), dim), (parts,), jnp.float32, low / len(pieces), high / len(pieces))
        factor_of = factor_of * jnp.repeat(jnp.exp(draws), dims[dim] // parts).reshape((-1,) + (1,) * (len(dims) - 1 - dim))
    return factor_of


def gaussian(own_key, extent, deviation, most, cuts=(), dtype=jnp.bfloat16):
    array = jax.random.normal(own_key, extent, jnp.float32) * deviation
    if len(cuts) > 0:
        array = block_scale(own_key, extent, cuts, -0.22, 0.18) * array
    return jnp.clip(array, min=-most, max=most).astype(dtype)


def setup_inputs(seed: int = 0, part: int = 0) -> dict:
    keys = jax.random.split(jax.random.key(seed), 14)
    own_keys = jax.random.split(jax.random.fold_in(keys[13], part), 14)
    return {
        "fields": gaussian(own_keys[0], (V, ROWS, COLS * PIX), 1.0, 6.0, ((0, 8), (1, 8))),
        "var_ids": jax.random.permutation(keys[1], V).astype(jnp.int32),
        "level_of": place_ends(jax.random.randint(keys[2], (V,), 0, NLEV), jax.random.fold_in(keys[2], 1), 0, NLEV - 1).astype(jnp.int32),
        "window_offset": jax.random.randint(own_keys[3], (1,), 0, LAT - ROWS + 1).astype(jnp.int32),
        "w_embed": gaussian(keys[4], (V, PIX, D), PIX ** -0.5, 1.5),
        "var_emb": gaussian(keys[5], (V, D), 1.0, 6.0),
        "w_key": gaussian(keys[6], (D, D), D ** -0.5, 0.25),
        "w_value": gaussian(keys[7], (D, D), D ** -0.5, 0.25),
        "w_out": gaussian(keys[8], (D, D), D ** -0.5, 0.25),
        "latent_query": gaussian(keys[9], (H, DH), 1.5, 9.0, (), jnp.float32),
        "bias_table": draw_bias_table(jax.random.fold_in(keys[13], 71), part),
        "lat_emb": gaussian(keys[11], (LAT, D), 0.5, 3.0),
        "d_aggregated": gaussian(own_keys[12], (ROWS, COLS, D), 1.0, 6.0, ((1, 64),)),
    }


def attend(tokens, bias_rows, latent_query, w_key, w_value, w_out, lat_rows, cotangent):
    var_count, patch_count, width = tokens.shape
    head_count, head_size = latent_query.shape
    score_scale = head_size ** (-0.5)
    flat_tokens = tokens.reshape(var_count * patch_count, width)
    key_rows = jnp.dot(flat_tokens, w_key, preferred_element_type=jnp.float32)
    key_heads = key_rows.reshape(var_count, patch_count, head_count, head_size)
    inverse_rms = lax.rsqrt(lax.optimization_barrier(jnp.mean(key_heads * key_heads, axis=-1, keepdims=True)) + 1e-06)
    normed = key_heads * inverse_rms
    scores = jnp.einsum('vphe,he->phv', normed, latent_query, precision=lax.Precision.HIGHEST) * score_scale + bias_rows.T[None]
    largest = lax.optimization_barrier(jnp.max(scores, axis=-1, keepdims=True))
    raised = jnp.exp(scores - largest)
    weights = raised / lax.optimization_barrier(jnp.sum(raised, axis=-1, keepdims=True))
    attn_rounded = weights.astype(jnp.bfloat16)
    mixed_rows = jnp.einsum('phv,vpd->phd', attn_rounded.astype(jnp.float32), tokens.astype(jnp.float32)).astype(jnp.bfloat16)
    value_heads = w_value.reshape(width, head_count, head_size)
    context = jnp.einsum('phd,dhe->phe', mixed_rows.astype(jnp.float32), value_heads.astype(jnp.float32)).astype(jnp.bfloat16).reshape(patch_count, width)
    output = (jnp.dot(context, w_out, preferred_element_type=jnp.float32) + lat_rows.astype(jnp.float32)).astype(jnp.bfloat16)
    grad_context = jnp.dot(cotangent, w_out.T, preferred_element_type=jnp.float32).astype(jnp.bfloat16)
    grad_heads = grad_context.reshape(patch_count, head_count, head_size)
    value_grad = jnp.einsum('phd,phe->dhe', mixed_rows.astype(jnp.float32), grad_heads.astype(jnp.float32)).reshape(width, width)
    grad_mixed = jnp.einsum('phe,dhe->phd', grad_heads.astype(jnp.float32), value_heads.astype(jnp.float32)).astype(jnp.bfloat16)
    grad_attn = jnp.einsum('phd,vpd->phv', grad_mixed.astype(jnp.float32), tokens.astype(jnp.float32))
    grad_scores = weights * (grad_attn - lax.optimization_barrier(jnp.sum(weights * grad_attn, axis=-1, keepdims=True)))
    grad_normed = jnp.einsum('phv,he->vphe', grad_scores, latent_query, precision=lax.Precision.HIGHEST) * score_scale
    grad_keys = (inverse_rms * (grad_normed - normed * lax.optimization_barrier(jnp.mean(grad_normed * normed, axis=-1, keepdims=True)))).astype(jnp.bfloat16)
    grad_keys = grad_keys.reshape(var_count * patch_count, width)
    key_grad = jnp.einsum('nd,ne->de', flat_tokens.astype(jnp.float32), grad_keys.astype(jnp.float32))
    through_keys = jnp.dot(grad_keys, w_key.T, preferred_element_type=jnp.float32).reshape(var_count, patch_count, width)
    through_values = jnp.einsum('phv,phd->vpd', attn_rounded.astype(jnp.float32), grad_mixed.astype(jnp.float32))
    token_grad = (through_values + through_keys).astype(jnp.bfloat16)
    return (output, token_grad, key_grad, value_grad)

def reference(fields, var_ids, level_of, window_offset, w_embed, var_emb, w_key, w_value, w_out, latent_query, bias_table, lat_emb, d_aggregated):
    w_rows = jnp.take(w_embed, var_ids, axis=0)
    emb_rows = jnp.take(var_emb, var_ids, axis=0)
    bias_rows = jnp.take(bias_table, jnp.take(level_of, var_ids, axis=0), axis=0)
    lat_rows = lax.dynamic_slice_in_dim(lat_emb, window_offset[0], ROWS, 0)
    columns = fields.reshape(V, ROWS, COLS, PIX).transpose(2, 0, 1, 3)
    cot_columns = d_aggregated.transpose(1, 0, 2)

    def column_step(totals, item):
        patches, cotangent = item
        tokens = (jnp.einsum('vpk,vkd->vpd', patches.astype(jnp.float32), w_rows.astype(jnp.float32)) + emb_rows[:, None, :].astype(jnp.float32)).astype(jnp.bfloat16)
        output, token_grad, key_grad, value_grad = attend(tokens, bias_rows, latent_query, w_key, w_value, w_out, lat_rows, cotangent)
        embed_part = jnp.einsum('vpk,vpd->vkd', patches.astype(jnp.float32), token_grad.astype(jnp.float32))
        var_part = lax.optimization_barrier(jnp.sum(token_grad.astype(jnp.float32), axis=1))
        return ((totals[0] + embed_part, totals[1] + var_part, totals[2] + key_grad, totals[3] + value_grad), output)
    start_sums = (jnp.zeros((V, PIX, D), jnp.float32), jnp.zeros((V, D), jnp.float32), jnp.zeros((D, D), jnp.float32), jnp.zeros((D, D), jnp.float32))
    totals, outputs = lax.scan(column_step, start_sums, (columns, cot_columns))
    return (outputs.transpose(1, 0, 2), totals[0], totals[1], totals[2], totals[3])
```

```python
import jax
import jax.numpy as jnp
from jax import lax
from jax.sharding import PartitionSpec as P


def local(
    fields,
    var_ids,
    level_of,
    window_offset,
    w_embed,
    var_emb,
    w_key,
    w_value,
    w_out,
    latent_query,
    bias_table,
    lat_emb,
    d_aggregated,
):
    f32, bf16 = jnp.float32, jnp.bfloat16
    nv, nr, merged = fields.shape
    pix, width = w_embed.shape[1:]
    heads, dh = latent_query.shape
    rows = d_aggregated.shape[0]
    cols = merged // pix
    npatch = nr * cols
    nvar, npat = lax.axis_size("var"), lax.axis_size("patch")
    i, j = lax.axis_index("var"), lax.axis_index("patch")
    ids = lax.dynamic_slice_in_dim(var_ids, i * nv, nv, 0)
    bias = jnp.take(bias_table, jnp.take(level_of, ids, axis=0), axis=0)
    wa = jnp.concatenate(
        [jnp.take(w_embed, ids, axis=0), jnp.take(var_emb, ids, axis=0)[:, None]], axis=1
    )
    wkv = jnp.concatenate([w_key, w_value], axis=1)
    we = jnp.einsum("vkd,de->vke", wa, wkv, preferred_element_type=f32).astype(bf16)
    f = fields.reshape(nv, npatch, pix).transpose(0, 2, 1)
    f = jnp.concatenate([f, jnp.ones((nv, 1, npatch), bf16)], axis=1)
    gc = jnp.dot(d_aggregated[:, 0], w_out.T, preferred_element_type=f32).astype(bf16)
    gc = lax.all_to_all(gc.reshape(npat, nr, width), "patch", 0, 0, tiled=True)
    gc = lax.all_gather(gc, "var")
    gc = gc.transpose(2, 0, 1, 3).reshape(npatch, width)
    gct = gc.astype(f32).T.reshape(heads, dh, npatch)
    kv = jnp.einsum("vke,vkp->vep", we, f, preferred_element_type=f32)
    keys = kv[:, :width].reshape(nv, heads, dh, npatch)
    vals = kv[:, width:].reshape(nv, heads, dh, npatch)
    inv = lax.rsqrt(jnp.mean(keys * keys, axis=2) + 1e-6)
    scale = dh**-0.5
    s0 = scale * inv * jnp.sum(keys * latent_query[None, :, :, None], axis=2)
    s = s0 + bias[:, :, None]
    ga = jnp.sum(vals * gct[None], axis=2)
    m = jnp.max(s, axis=0)
    e = jnp.exp(s - m)
    l = jnp.sum(e, axis=0)
    r = jnp.sum(e * ga, axis=0)
    ctx = jnp.sum(e[:, :, None] * vals, axis=0)
    stats = lax.all_gather(jnp.stack([m, l, r]), "var")
    mall = jnp.max(stats[:, 0], axis=0)
    fac = jnp.exp(stats[:, 0] - mall)
    lall = jnp.sum(fac * stats[:, 1], axis=0)
    rall = jnp.sum(fac * stats[:, 2], axis=0) / lall
    own = jnp.exp(m - mall) / lall
    ctx = ctx * own[:, None]
    ctx = ctx.reshape(width, nr, nvar, npat).transpose(2, 1, 3, 0)
    ctx = lax.psum_scatter(ctx, "var", scatter_dimension=0)
    ctx = ctx.reshape(nr, npat, width).astype(bf16)
    row0 = window_offset[0] + j * nr
    lat = lax.dynamic_slice_in_dim(lat_emb, row0, nr, 0).astype(f32)
    out = jnp.einsum("rpd,de->rpe", ctx, w_out, preferred_element_type=f32) + lat[:, None]
    out = lax.all_to_all(out.astype(bf16), "patch", 1, 0, tiled=True)
    out = out.reshape(rows, 1, width)
    attn = e * own
    gs = attn * (ga - rall)
    ca = scale * inv * gs
    cb = -inv * inv * gs * s0 / dh
    gk = ca[:, :, None] * latent_query[None, :, :, None] + cb[:, :, None] * keys
    ag = attn[:, :, None] * gct[None]
    g = jnp.concatenate(
        [gk.reshape(nv, width, npatch), ag.reshape(nv, width, npatch)], axis=1
    ).astype(bf16)
    fg = jnp.einsum("vkp,vep->vke", f, g, preferred_element_type=f32).astype(bf16)
    eg = jnp.einsum("vke,de->vkd", fg, wkv, preferred_element_type=f32).astype(bf16)
    kvg = jnp.einsum("vkd,vke->de", wa, fg, preferred_element_type=f32)
    eg = lax.psum(eg, "patch").astype(f32)
    kvg = lax.psum(kvg, ("var", "patch"))
    return out, eg[:, :pix], eg[:, pix], kvg[:, :width], kvg[:, width:]


def solution(mesh):
    split = P(("win", "var"), "patch", None)
    column = P("win", ("var", "patch"), None)
    in_specs = (split, P(), P(), P("win")) + (P(),) * 8 + (column,)
    out_specs = (
        column,
        P(("win", "var"), None, None),
        P(("win", "var"), None),
        P("win", None),
        P("win", None),
    )
    return jax.shard_map(local, mesh=mesh, in_specs=in_specs, out_specs=out_specs, check_vma=False)
```

```python
import jax
import jax.numpy as jnp
from jax import lax
from jax.experimental import pallas as pl
from jax.experimental.pallas import tpu as pltpu
from jax.sharding import PartitionSpec as P

f32, bf16, i32 = jnp.float32, jnp.bfloat16, jnp.int32
NV, VL, PIX, D, H, DH, NP = 30, 15, 16, 512, 8, 64, 128
GR = 256
NN = (((1,), (0,)), ((), ()))
NT = (((1,), (1,)), ((), ()))


def iota(shape, dim):
    return lax.broadcasted_iota(i32, shape, dim)


def dot(a, b, dims=NN):
    return lax.dot_general(a, b, dims, preferred_element_type=f32)


def split(x):
    hi = x.astype(bf16)
    return hi, (x - hi.astype(f32)).astype(bf16)


def var_of(row):
    return jnp.where(row < VL * PIX, row >> 4, row - VL * PIX)


def kernel(
    ids_s, lvl_s, off_s, bias_s,
    fields_h, we_h, ve_h, wk_h, wv_h, wo_h, q_v, lat_v, d_h,
    agg_o, eg_o, kv_o,
    fld, wem, vem, wk, wv, wo, lsem,
    x_buf, x_ss, x_rs,
    g_snd, g_buf, g_ss, g_rs,
    st_buf, st_ss, st_rs,
    c_snd, c_buf, c_ss, c_rs,
    a_snd, a_buf, a_ss, a_rs,
    kvb, rk1, rk2, rk3, s1, s2, fink,
    egb, re1, re2, e1, fine,
    k_ss, k_rs, e_ss, e_rs,
    wa, wat, wek, wev, wekt, wevt, ff, fb, bi, ss, sn, ga, gc, at, ca, cb, eb, fg, ctxt,
):
    i, j = lax.axis_index("var"), lax.axis_index("patch")
    z, xh = i // 2, i % 2
    y, c = j // 2, j % 2
    q_me = y * 2 + xh

    def remote(src, dst, ssem, rsem, **dev):
        return pltpu.make_async_remote_copy(
            src_ref=src,
            dst_ref=dst,
            send_sem=ssem,
            recv_sem=rsem,
            device_id=dev,
            device_id_type=pl.DeviceIdType.MESH,
        )

    local = [
        pltpu.make_async_copy(src, dst, lsem.at[n])
        for n, (src, dst) in enumerate(
            [
                (fields_h, fld),
                (we_h, wem),
                (ve_h, vem.at[pl.ds(0, 240)]),
                (wk_h, wk),
                (wv_h, wv),
                (wo_h, wo),
                (d_h, x_buf.at[i]),
            ]
        )
    ]
    for cp in local:
        cp.start()

    barrier = pltpu.get_barrier_semaphore()
    peers = [dict(var=(i + t) % 8) for t in range(1, 8)]
    peers += [dict(patch=(j + t) % 8) for t in range(1, 8)]
    peers += [dict(var=z * 2 + 1 - xh, patch=((y + t) % 4) * 2 + c) for t in range(1, 4)]
    for dev in peers:
        pl.semaphore_signal(barrier, inc=1, device_id=dev, device_id_type=pl.DeviceIdType.MESH)
    pl.semaphore_wait(barrier, len(peers))

    xs = [remote(d_h, x_buf.at[i], x_ss.at[t - 1], x_rs.at[t - 1], var=(i + t) % 8) for t in range(1, 8)]
    for cp in xs:
        cp.start()

    def bias_step(v, _):
        lvl = lvl_s[ids_s[i * NV + v]]
        slot = v + v // VL
        for h in range(H):
            bi[h, pl.ds(slot, 1), :] = jnp.full((1, NP), bias_s[lvl, h], f32)
        return 0

    lax.fori_loop(0, NV, bias_step, 0)

    local[0].wait()
    lane_col = iota((8, NP), 1) >> 4
    own = lane_col == iota((8, NP), 0)
    pick = ((iota((PIX, NP), 1) & 15) == iota((PIX, NP), 0)).astype(bf16)
    for g in range(2):
        parts = []
        for v in range(VL):
            row = fld[g * VL + v].astype(f32)
            for b in range(8):
                for r in range(2):
                    piece = jnp.broadcast_to(row[r : r + 1, b * 128 : (b + 1) * 128], (8, 128))
                    parts.append(jnp.where(own, piece, 0.0))
        spread = jnp.concatenate(parts, axis=0).astype(bf16)
        ft = dot(pick, spread, NT)
        for v in range(VL):
            ff[g, v * PIX : (v + 1) * PIX, :] = ft[:, v * NP : (v + 1) * NP]
        ff[g, VL * PIX :, :] = jnp.where(iota((16, NP), 0) < VL, 1.0, 0.0)
        fb[g] = ff[g].astype(bf16)

    local[1].wait()

    def gather_step(v, _):
        g = v // VL
        row = pl.multiple_of(g * GR + (v - g * VL) * PIX, PIX)
        wa[pl.ds(row, PIX), :] = wem[ids_s[i * NV + v]]
        return 0

    lax.fori_loop(0, NV, gather_step, 0)
    vem[240:, :] = jnp.zeros((16, D), bf16)
    local[2].wait()
    for g in range(2):
        want = jnp.full((16, 256), -1, i32)
        for v in range(VL):
            want = jnp.where(iota((16, 256), 0) == v, ids_s[i * NV + g * VL + v], want)
        hot = jnp.where(want == iota((16, 256), 1), 1.0, 0.0).astype(bf16)
        wa[g * GR + VL * PIX : (g + 1) * GR, :] = dot(hot, vem[...]).astype(bf16)
    local[3].wait()
    local[4].wait()
    wat[...] = wa[...].T
    wek[...] = dot(wa[...], wk[...]).astype(bf16)
    wev[...] = dot(wa[...], wv[...]).astype(bf16)
    for g in range(2):
        wekt[g] = wek[g * GR : (g + 1) * GR, :].T
        wevt[g] = wev[g * GR : (g + 1) * GR, :].T

    local[5].wait()
    local[6].wait()
    for cp in xs:
        cp.wait()
    gx = dot(x_buf[...].reshape(NP, D), wo[...], NT).astype(bf16)
    o = iota((NP, NP), 0)
    src = ((o >> 1) & 7) * 16 + (o >> 4) * 2 + (o & 1)
    perm = jnp.where(src == iota((NP, NP), 1), 1.0, 0.0).astype(bf16)
    gs_rows = dot(perm, gx).astype(bf16)
    g_snd[...] = gs_rows.reshape(8, 16, D)
    gsends = []
    for t in range(1, 8):
        peer = (j + t) % 8
        gsends.append(remote(g_snd.at[peer], g_buf.at[j], g_ss.at[t - 1], g_rs.at[t - 1], patch=peer))
    for cp in gsends:
        cp.start()
    g_buf[j] = g_snd[j]

    spread_q = jnp.where((iota((DH, D), 1) & 63) == iota((DH, D), 0), 1.0, 0.0)
    qall = jnp.dot(q_v[...], spread_q, precision=lax.Precision.HIGHEST, preferred_element_type=f32)
    qblk = jnp.where((iota((H, D), 1) >> 6) == iota((H, D), 0), qall, 0.0)
    qrow = jnp.sum(qblk, axis=0, keepdims=True)
    wq = dot(jnp.concatenate(split(qblk), axis=0), wk[...], NT)
    wq = wq[:H] + wq[H:]
    aq = dot(jnp.concatenate(split(wq), axis=0), wa[...], NT)
    aq = aq[:H] + aq[H:]
    lane_var = var_of(iota((16, GR), 1))
    member = lane_var == iota((16, GR), 0)
    sums = jnp.where(member, 1.0, 0.0).astype(bf16)
    for g in range(2):
        rows = [
            jnp.where(member, jnp.broadcast_to(aq[h : h + 1, g * GR : (g + 1) * GR], (16, GR)), 0.0)
            for h in range(H)
        ]
        hi, lo = split(jnp.concatenate(rows, axis=0))
        got = dot(hi, fb[g]) + dot(lo, fb[g])
        for h in range(H):
            sn[h, g * 16 : (g + 1) * 16, :] = got[h * 16 : (h + 1) * 16]

    heads = jnp.where((iota((16, D), 1) >> 6) == iota((16, D), 0), 1.0, 0.0).astype(bf16)
    tile_row = iota((16, NP), 0)
    for g in range(2):
        ones = ff[g, VL * PIX :, :]
        for t in range(8):
            cols = []
            for v in (2 * t, 2 * t + 1):
                top = []
                if v < VL:
                    if v > 0:
                        top.append(jnp.zeros((v * PIX, NP), bf16))
                    top.append(fb[g, v * PIX : (v + 1) * PIX, :])
                    if v < VL - 1:
                        top.append(jnp.zeros(((VL - 1 - v) * PIX, NP), bf16))
                else:
                    top.append(jnp.zeros((VL * PIX, NP), bf16))
                top.append(jnp.where(tile_row == v, ones, 0.0).astype(bf16))
                cols.append(jnp.concatenate(top, axis=0))
            keys = dot(wekt[g], jnp.concatenate(cols, axis=1))
            sq = dot(heads, (keys * keys).astype(bf16))
            ss[:, g * 16 + 2 * t, :] = sq[:H, :NP]
            ss[:, g * 16 + 2 * t + 1, :] = sq[:H, NP:]

    scale = DH**-0.5
    slot = iota((H, 32, NP), 1)
    real = (slot & 15) < VL
    inv = lax.rsqrt(ss[...] * (1.0 / DH) + 1e-6)
    s0 = scale * inv * sn[...]
    s = jnp.where(real, s0 + bi[...], -1e30)
    m = jnp.max(s, axis=1, keepdims=True)
    e = jnp.where(real, jnp.exp(s - m), 0.0)
    at[...] = e
    st_buf[i, 0] = m[:, 0, :]
    st_buf[i, 1] = jnp.sum(e, axis=1)
    sn[...] = s0
    ss[...] = inv

    for cp in gsends:
        cp.wait()
    o = iota((NP, NP), 0)
    src = (o & 7) * 16 + (o >> 4) * 2 + ((o >> 3) & 1)
    perm = jnp.where(src == iota((NP, NP), 1), 1.0, 0.0).astype(bf16)
    gcf = dot(perm, g_buf[...].reshape(NP, D))
    gc[...] = gcf.astype(bf16)
    gct = gcf.T
    top_half = iota((NP, NP), 0) < DH
    for pair in range(4):
        piece = gct[pair * 128 : (pair + 1) * 128]
        blocks = jnp.concatenate(
            [jnp.where(top_half, piece, 0.0), jnp.where(top_half, 0.0, piece)], axis=1
        ).astype(bf16)
        for g in range(2):
            prod = dot(wev[g * GR : (g + 1) * GR, pair * 128 : (pair + 1) * 128], blocks)
            fg_rows = ff[g]
            hi, lo = split(prod * jnp.concatenate([fg_rows, fg_rows], axis=1))
            got = dot(sums, hi) + dot(sums, lo)
            ga[2 * pair, g * 16 : (g + 1) * 16, :] = got[:, :NP]
            ga[2 * pair + 1, g * 16 : (g + 1) * 16, :] = got[:, NP:]
    st_buf[i, 2] = jnp.sum(at[...] * ga[...], axis=1)
    sts = [
        remote(st_buf.at[i], st_buf.at[i], st_ss.at[t - 1], st_rs.at[t - 1], var=(i + t) % 8)
        for t in range(1, 8)
    ]
    for cp in sts:
        cp.start()
    for cp in sts:
        cp.wait()
    mall = st_buf[0, 0]
    for n in range(1, 8):
        mall = jnp.maximum(mall, st_buf[n, 0])
    lall = jnp.zeros((H, NP), f32)
    rall = jnp.zeros((H, NP), f32)
    for n in range(8):
        fac = jnp.exp(st_buf[n, 0] - mall)
        lall = lall + fac * st_buf[n, 1]
        rall = rall + fac * st_buf[n, 2]
    rall = rall / lall
    mine = jnp.exp(st_buf[i, 0] - mall) / lall
    attn = at[...] * mine[:, None, :]
    inv = ss[...]
    gs = attn * (ga[...] - rall[:, None, :])
    at[...] = attn
    ca[...] = scale * inv * gs
    cb[...] = (-1.0 / DH) * inv * inv * gs * sn[...]

    def times_fields(ref, h, g):
        x = ref[h, g * 16 : (g + 1) * 16, :]
        parts = [jnp.broadcast_to(x[v : v + 1], (PIX, NP)) for v in range(VL)] + [x]
        return (jnp.concatenate(parts, axis=0) * ff[g]).astype(bf16)

    low = iota((NP, 128), 1) < DH
    lowg = iota((GR, 128), 1) < DH
    zero = jnp.zeros((), bf16)
    for pair in range(4):
        lanes = slice(pair * 128, (pair + 1) * 128)
        piece = gc[:, lanes].astype(f32)
        gd = jnp.concatenate([jnp.where(low, piece, 0.0), jnp.where(low, 0.0, piece)], axis=0)
        gd = gd.astype(bf16)
        for g in range(2):
            pieces = []
            for n in range(2):
                x = times_fields(at, 2 * pair + n, g)
                eb[2 * pair + n, g * GR : (g + 1) * GR, :] = x
                pieces.append(x)
            fg[g * GR : (g + 1) * GR, D + pair * 128 : D + (pair + 1) * 128] = dot(
                jnp.concatenate(pieces, axis=1), gd
            ).astype(bf16)
    kvb[D:, :] = dot(wat[...], fg[:, D:]).astype(bf16)

    same = var_of(iota((GR, GR), 0)) == var_of(iota((GR, GR), 1))
    for pair in range(4):
        lanes = slice(pair * 128, (pair + 1) * 128)
        qp = jnp.broadcast_to(qrow[:, lanes], (NP, 128))
        qd = jnp.concatenate([jnp.where(low, qp, 0.0), jnp.where(low, 0.0, qp)], axis=0).astype(bf16)
        for g in range(2):
            wp = wek[g * GR : (g + 1) * GR, lanes].astype(f32)
            wd = jnp.concatenate([jnp.where(lowg, wp, 0.0), jnp.where(lowg, 0.0, wp)], axis=0)
            wd = wd.astype(bf16)
            af, ms = [], []
            for n in range(2):
                af.append(times_fields(ca, 2 * pair + n, g))
                mm = dot(times_fields(cb, 2 * pair + n, g), fb[g], NT)
                ms.append(jnp.where(same, mm, 0.0).astype(bf16))
            total = dot(jnp.concatenate(af, axis=1), qd) + dot(jnp.concatenate(ms, axis=1), wd)
            fg[g * GR : (g + 1) * GR, lanes] = total.astype(bf16)
    kvb[:D, :] = dot(wat[...], fg[:, :D]).astype(bf16)

    sib = y * 2 + 1 - c
    k1 = remote(kvb.at[pl.ds((1 - c) * D, D)], rk1, k_ss.at[0], k_rs.at[0], patch=sib)
    k1.start()
    for g in range(2):
        rows = slice(g * GR, (g + 1) * GR)
        egb[rows, :] = (dot(fg[rows, :D], wk[...], NT) + dot(fg[rows, D:], wv[...], NT)).astype(bf16)
    ex1 = remote(egb.at[pl.ds((1 - c) * GR, GR)], re1, e_ss.at[0], e_rs.at[0], patch=sib)
    ex1.start()

    for h in range(H):
        acc = dot(wevt[0, h * DH : (h + 1) * DH, :], eb[h, :GR, :])
        acc = acc + dot(wevt[1, h * DH : (h + 1) * DH, :], eb[h, GR:, :])
        ctxt[h * DH : (h + 1) * DH, :] = acc
    c_snd[...] = ctxt[...].T.astype(bf16).reshape(8, 16, D)
    cs = []
    for t in range(1, 8):
        peer = (i + t) % 8
        cs.append(remote(c_snd.at[peer], c_buf.at[i], c_ss.at[t - 1], c_rs.at[t - 1], var=peer))
    for cp in cs:
        cp.start()
    c_buf[i] = c_snd[i]

    k1.wait()
    s1[...] = (kvb[pl.ds(c * D, D), :].astype(f32) + rk1[...].astype(f32)).astype(bf16)
    k2 = []
    for t in range(1, 4):
        peer = (z + t) % 4
        k2.append(
            remote(s1.at[pl.ds(peer * 128, 128)], rk2.at[t - 1], k_ss.at[t], k_rs.at[t], var=peer * 2 + xh)
        )
    for cp in k2:
        cp.start()
    ex1.wait()
    e1[...] = (egb[pl.ds(c * GR, GR), :].astype(f32) + re1[...].astype(f32)).astype(bf16)
    ex2 = []
    for t in range(1, 4):
        peer = (y + t) % 4
        ex2.append(
            remote(e1.at[pl.ds(peer * 64, 64)], re2.at[t - 1], e_ss.at[t], e_rs.at[t], patch=peer * 2 + c)
        )
    for cp in ex2:
        cp.start()

    for cp in cs:
        cp.wait()
    cx = c_buf[0].astype(f32)
    for n in range(1, 8):
        cx = cx + c_buf[n].astype(f32)
    row = off_s[0] + 2 * j + (iota((16, 180), 0) >> 3)
    hot = jnp.where(row == iota((16, 180), 1), 1.0, 0.0).astype(bf16)
    agg = (dot(cx.astype(bf16), wo[...]) + dot(hot, lat_v[...])).astype(bf16)
    dst = iota((NP, 16), 0)
    r = (dst & 15) - 2 * j
    take = ((r >= 0) & (r < 2)) & (iota((NP, 16), 1) == r * 8 + (dst >> 4))
    a_snd[...] = dot(jnp.where(take, 1.0, 0.0).astype(bf16), agg).astype(bf16).reshape(8, 16, D)
    sends = []
    for t in range(1, 8):
        peer = (j + t) % 8
        sends.append(remote(a_snd.at[peer], a_buf.at[j], a_ss.at[t - 1], a_rs.at[t - 1], patch=peer))
    for cp in sends:
        cp.start()
    a_buf[j] = a_snd[j]

    for cp in k2:
        cp.wait()
    tot = s1[pl.ds(z * 128, 128), :].astype(f32)
    for n in range(3):
        tot = tot + rk2[n].astype(f32)
    s2[...] = tot.astype(bf16)
    k3 = []
    for t in range(1, 8):
        q = (q_me + t) % 8
        k3.append(
            remote(
                s2.at[pl.ds(q * 16, 16)], rk3.at[t - 1], k_ss.at[3 + t], k_rs.at[3 + t],
                var=z * 2 + q % 2, patch=(q // 2) * 2 + c,
            )
        )
    for cp in k3:
        cp.start()
    for cp in ex2:
        cp.wait()
    tot = e1[pl.ds(y * 64, 64), :].astype(f32)
    for n in range(3):
        tot = tot + re2[n].astype(f32)
    erow = c * GR + y * 64
    fine[pl.ds(erow, 64), :] = tot.astype(bf16)
    ex3 = []
    for t in range(1, 4):
        peer = (y + t) % 4
        own_rows = fine.at[pl.ds(erow, 64)]
        ex3.append(remote(own_rows, own_rows, e_ss.at[3 + t], e_rs.at[3 + t], patch=peer * 2 + c))
    for cp in ex3:
        cp.start()
    for cp in k3:
        cp.wait()
    tot = s2[pl.ds(q_me * 16, 16), :].astype(f32)
    for n in range(7):
        tot = tot + rk3[n].astype(f32)
    krow = c * D + z * 128
    own_rows = fink.at[pl.ds(krow + q_me * 16, 16)]
    fink[pl.ds(krow + q_me * 16, 16), :] = tot.astype(bf16)
    k4 = []
    for t in range(1, 8):
        q = (q_me + t) % 8
        k4.append(
            remote(
                own_rows, own_rows, k_ss.at[10 + t], k_rs.at[10 + t],
                var=z * 2 + q % 2, patch=(q // 2) * 2 + c,
            )
        )
    for cp in k4:
        cp.start()
    for cp in ex3:
        cp.wait()
    half = fine.at[pl.ds(c * GR, GR)]
    ex4 = remote(half, half, e_ss.at[7], e_rs.at[7], patch=sib)
    ex4.start()
    for cp in k4:
        cp.wait()
    k5 = []
    for t in range(1, 4):
        peer = (z + t) % 4
        part = fink.at[pl.ds(krow, 128)]
        k5.append(remote(part, part, k_ss.at[17 + t], k_rs.at[17 + t], var=peer * 2 + xh))
    for cp in k5:
        cp.start()

    for cp in sends:
        cp.wait()
    acc = a_buf[0].astype(f32)
    for n in range(1, 8):
        acc = acc + a_buf[n].astype(f32)
    a_snd[0] = acc.astype(bf16)
    outs = [pltpu.make_async_copy(a_snd.at[0], agg_o, lsem.at[7])]
    outs[0].start()
    ex4.wait()
    outs.append(pltpu.make_async_copy(fine, eg_o, lsem.at[8]))
    outs[1].start()
    for cp in k5:
        cp.wait()
    half = fink.at[pl.ds(c * D, D)]
    k6 = remote(half, half, k_ss.at[21], k_rs.at[21], patch=sib)
    k6.start()
    k6.wait()
    outs.append(pltpu.make_async_copy(fink, kv_o, lsem.at[9]))
    outs[2].start()
    for cp in outs:
        cp.wait()


def local(fields, var_ids, level_of, window_offset, w_embed, var_emb, w_key, w_value, w_out,
          latent_query, bias_table, lat_emb, d_aggregated):
    smem = pl.BlockSpec(memory_space=pltpu.SMEM)
    vmem = pl.BlockSpec(memory_space=pltpu.VMEM)
    hbm = pl.BlockSpec(memory_space=pl.ANY)
    dma = pltpu.SemaphoreType.DMA

    def v(*shape, dtype=bf16):
        return pltpu.VMEM(shape, dtype)

    scratch = [
        v(NV, 2, 1024), v(240, PIX, D), v(256, D), v(D, D), v(D, D), v(D, D), dma((10,)),
        v(8, 16, D), dma((7,)), dma((7,)),
        v(8, 16, D), v(8, 16, D), dma((7,)), dma((7,)),
        v(8, 3, H, NP, dtype=f32), dma((7,)), dma((7,)),
        v(8, 16, D), v(8, 16, D), dma((7,)), dma((7,)),
        v(8, 16, D), v(8, 16, D), dma((7,)), dma((7,)),
        v(2 * D, D), v(D, D), v(3, 128, D), v(7, 16, D), v(D, D), v(128, D), v(2 * D, D),
        v(D, D), v(GR, D), v(3, 64, D), v(GR, D), v(D, D),
        dma((22,)), dma((22,)), dma((8,)), dma((8,)),
        v(D, D), v(D, D), v(D, D), v(D, D), v(2, D, GR), v(2, D, GR),
        v(2, GR, NP, dtype=f32), v(2, GR, NP),
    ]
    scratch += [v(H, 32, NP, dtype=f32)] * 4 + [v(NP, D)] + [v(H, 32, NP, dtype=f32)] * 3
    scratch += [v(H, D, NP), v(D, 2 * D), v(D, NP, dtype=f32)]
    agg, eg, kv = pl.pallas_call(
        kernel,
        out_shape=[
            jax.ShapeDtypeStruct((16, D), bf16),
            jax.ShapeDtypeStruct((D, D), bf16),
            jax.ShapeDtypeStruct((2 * D, D), bf16),
        ],
        in_specs=[smem] * 4 + [hbm] * 6 + [vmem] * 2 + [hbm],
        out_specs=[hbm] * 3,
        scratch_shapes=scratch,
        compiler_params=pltpu.CompilerParams(
            collective_id=0, has_side_effects=True, vmem_limit_bytes=48 * 1024 * 1024
        ),
    )(
        var_ids, level_of, window_offset, bias_table,
        fields, w_embed, var_emb, w_key, w_value, w_out, latent_query, lat_emb,
        d_aggregated.reshape(16, D),
    )
    eg = eg.reshape(2, GR, D)
    embed = eg[:, : VL * PIX].astype(f32).reshape(NV, PIX, D)
    var = eg[:, VL * PIX : GR - 1].astype(f32).reshape(NV, D)
    kv = kv.astype(f32)
    return agg.reshape(16, 1, D), embed, var, kv[:D], kv[D:]


def solution(mesh):
    split_rows = P(("win", "var"), "patch", None)
    column = P("win", ("var", "patch"), None)
    in_specs = (split_rows, P(), P(), P("win")) + (P(),) * 8 + (column,)
    out_specs = (
        column,
        P(("win", "var"), None, None),
        P(("win", "var"), None),
        P("win", None),
        P("win", None),
    )
    return jax.shard_map(local, mesh=mesh, in_specs=in_specs, out_specs=out_specs, check_vma=False)
```

```python
import jax
import jax.numpy as jnp
from jax import lax
from jax.experimental import pallas as pl
from jax.experimental.pallas import tpu as pltpu
from jax.sharding import PartitionSpec as P

f32, bf16, i32 = jnp.float32, jnp.bfloat16, jnp.int32
NV, VL, PIX, D, H, DH, NP = 30, 15, 16, 512, 8, 64, 128
GR = 256
NN = (((1,), (0,)), ((), ()))
NT = (((1,), (1,)), ((), ()))


def iota(shape, dim):
    return lax.broadcasted_iota(i32, shape, dim)


def dot(a, b, dims=NN):
    return lax.dot_general(a, b, dims, preferred_element_type=f32)


def split(x):
    hi = x.astype(bf16)
    return hi, (x - hi.astype(f32)).astype(bf16)


def var_of(row):
    return jnp.where(row < VL * PIX, row >> 4, row - VL * PIX)


def kernel(
    ids_h, lvl_h, off_h, bias_h,
    fields_h, we_h, ve_h, wk_h, wv_h, wo_h, q_h, lat_h, d_h,
    agg_o, eg_o, kg_o, vg_o,
    ids_s, lvl_s, off_s, bias_s, q_v, lat_v, fld, wem, vem, wk, wv, wo, lsem,
    x_buf, x_ss, x_rs,
    g_snd, g_buf, g_ss, g_rs,
    ml_buf, ml_ss, ml_rs,
    r_buf, r_ss, r_rs,
    c_snd, c_buf, c_ss, c_rs,
    a_snd, a_buf, a_ss, a_rs,
    kb, kr1, kr2, kr3, ks1, ks2, kfin,
    vb, vr1, vr2, vr3, vs1, vs2, vfin,
    egb, re1, re2, e1, fine,
    k_ss, k_rs, v_ss, v_rs, e_ss, e_rs,
    wa, wat, wek, wev, wekt, wevt, ff, fb, bi, ss, sn, ga, gc, at, ca, cb, eb, fg, ctxt,
):
    i, j = lax.axis_index("var"), lax.axis_index("patch")
    z, xh = i // 2, i % 2
    y, c = j // 2, j % 2
    w_me = z * 4 + y

    pending = []

    class Tr:
        def __init__(self, cp):
            self.cp = cp

        def start(self):
            self.cp.start()
            pending.append(self)

        def wait(self):
            self.cp.wait()
            pending.remove(self)

    def remote(src, dst, ssem, rsem, **dev):
        return Tr(pltpu.make_async_remote_copy(
            src_ref=src,
            dst_ref=dst,
            send_sem=ssem,
            recv_sem=rsem,
            device_id=dev,
            device_id_type=pl.DeviceIdType.MESH,
        ))

    local = [
        Tr(pltpu.make_async_copy(src, dst, lsem.at[n]))
        for n, (src, dst) in enumerate(
            [
                (fields_h, fld),
                (we_h, wem),
                (ve_h, vem.at[pl.ds(0, 240)]),
                (wk_h, wk),
                (wv_h, wv),
                (wo_h, wo),
                (d_h, x_buf.at[i]),
                (ids_h, ids_s),
                (lvl_h, lvl_s),
                (off_h, off_s),
                (bias_h, bias_s),
                (q_h, q_v),
                (lat_h, lat_v),
            ]
        )
    ]
    for cp in local:
        cp.start()

    barrier = pltpu.get_barrier_semaphore()
    peers = [dict(var=(i + t) % 8) for t in range(1, 8)]
    peers += [dict(patch=(j + t) % 8) for t in range(1, 8)]
    peers += [
        dict(var=((z + t) % 4) * 2 + xh, patch=((y + n) % 4) * 2 + c)
        for t in range(1, 4)
        for n in range(1, 4)
    ]
    for dev in peers:
        pl.semaphore_signal(barrier, inc=1, device_id=dev, device_id_type=pl.DeviceIdType.MESH)
    pl.semaphore_wait(barrier, len(peers))

    xs = [remote(d_h, x_buf.at[i], x_ss.at[t - 1], x_rs.at[t - 1], var=(i + t) % 8) for t in range(1, 8)]
    for cp in xs:
        cp.start()

    for n in range(7, 13):
        local[n].wait()
    def bias_step(v, _):
        lvl = lvl_s[ids_s[i * NV + v]]
        slot = v + v // VL
        for h in range(H):
            bi[h, pl.ds(slot, 1), :] = jnp.full((1, NP), bias_s[h, lvl], f32)
        return 0

    lax.fori_loop(0, NV, bias_step, 0)

    local[0].wait()
    lane_col = iota((8, NP), 1) >> 4
    own = lane_col == iota((8, NP), 0)
    pick = ((iota((PIX, NP), 1) & 15) == iota((PIX, NP), 0)).astype(bf16)
    for g in range(2):
        parts = []
        for v in range(VL):
            row = fld[g * VL + v].astype(f32)
            for b in range(8):
                for r in range(2):
                    piece = jnp.broadcast_to(row[r : r + 1, b * 128 : (b + 1) * 128], (8, 128))
                    parts.append(jnp.where(own, piece, 0.0))
        spread = jnp.concatenate(parts, axis=0).astype(bf16)
        ft = dot(pick, spread, NT)
        for v in range(VL):
            ff[g, v * PIX : (v + 1) * PIX, :] = ft[:, v * NP : (v + 1) * NP]
        ff[g, VL * PIX :, :] = jnp.where(iota((16, NP), 0) < VL, 1.0, 0.0)
        fb[g] = ff[g].astype(bf16)

    local[1].wait()

    def gather_step(v, _):
        g = v // VL
        row = pl.multiple_of(g * GR + (v - g * VL) * PIX, PIX)
        wa[pl.ds(row, PIX), :] = wem[ids_s[i * NV + v]]
        return 0

    lax.fori_loop(0, NV, gather_step, 0)
    vem[240:, :] = jnp.zeros((16, D), bf16)
    local[2].wait()
    for g in range(2):
        want = jnp.full((16, 256), -1, i32)
        for v in range(VL):
            want = jnp.where(iota((16, 256), 0) == v, ids_s[i * NV + g * VL + v], want)
        hot = jnp.where(want == iota((16, 256), 1), 1.0, 0.0).astype(bf16)
        wa[g * GR + VL * PIX : (g + 1) * GR, :] = dot(hot, vem[...]).astype(bf16)
    local[3].wait()
    local[4].wait()
    wat[...] = wa[...].T
    wek[...] = dot(wa[...], wk[...]).astype(bf16)
    wev[...] = dot(wa[...], wv[...]).astype(bf16)
    for g in range(2):
        wekt[g] = wek[g * GR : (g + 1) * GR, :].T
        wevt[g] = wev[g * GR : (g + 1) * GR, :].T

    local[5].wait()
    local[6].wait()
    for cp in xs:
        cp.wait()
    gx = dot(x_buf[...].reshape(NP, D), wo[...], NT).astype(bf16)
    o = iota((NP, NP), 0)
    src = ((o >> 1) & 7) * 16 + (o >> 4) * 2 + (o & 1)
    perm = jnp.where(src == iota((NP, NP), 1), 1.0, 0.0).astype(bf16)
    gs_rows = dot(perm, gx).astype(bf16)
    g_snd[...] = gs_rows.reshape(8, 16, D)
    gsends = []
    for t in range(1, 8):
        peer = (j + t) % 8
        gsends.append(remote(g_snd.at[peer], g_buf.at[j], g_ss.at[t - 1], g_rs.at[t - 1], patch=peer))
    for cp in gsends:
        cp.start()
    g_buf[j] = g_snd[j]

    spread_q = jnp.where((iota((DH, D), 1) & 63) == iota((DH, D), 0), 1.0, 0.0)
    qall = jnp.dot(q_v[...], spread_q, precision=lax.Precision.HIGHEST, preferred_element_type=f32)
    qblk = jnp.where((iota((H, D), 1) >> 6) == iota((H, D), 0), qall, 0.0)
    qrow = jnp.sum(qblk, axis=0, keepdims=True)
    wq = dot(jnp.concatenate(split(qblk), axis=0), wk[...], NT)
    wq = wq[:H] + wq[H:]
    aq = dot(jnp.concatenate(split(wq), axis=0), wa[...], NT)
    aq = aq[:H] + aq[H:]
    lane_var = var_of(iota((16, GR), 1))
    member = lane_var == iota((16, GR), 0)
    sums = jnp.where(member, 1.0, 0.0).astype(bf16)
    for g in range(2):
        rows = [
            jnp.where(member, jnp.broadcast_to(aq[h : h + 1, g * GR : (g + 1) * GR], (16, GR)), 0.0)
            for h in range(H)
        ]
        hi, lo = split(jnp.concatenate(rows, axis=0))
        got = dot(hi, fb[g]) + dot(lo, fb[g])
        for h in range(H):
            sn[h, g * 16 : (g + 1) * 16, :] = got[h * 16 : (h + 1) * 16]

    heads = jnp.where((iota((16, D), 1) >> 6) == iota((16, D), 0), 1.0, 0.0).astype(bf16)
    tile_row = iota((16, NP), 0)
    for g in range(2):
        ones = ff[g, VL * PIX :, :]
        for t in range(8):
            cols = []
            for v in (2 * t, 2 * t + 1):
                top = []
                if v < VL:
                    if v > 0:
                        top.append(jnp.zeros((v * PIX, NP), bf16))
                    top.append(fb[g, v * PIX : (v + 1) * PIX, :])
                    if v < VL - 1:
                        top.append(jnp.zeros(((VL - 1 - v) * PIX, NP), bf16))
                else:
                    top.append(jnp.zeros((VL * PIX, NP), bf16))
                top.append(jnp.where(tile_row == v, ones, 0.0).astype(bf16))
                cols.append(jnp.concatenate(top, axis=0))
            keys = dot(wekt[g], jnp.concatenate(cols, axis=1))
            sq = dot(heads, (keys * keys).astype(bf16))
            ss[:, g * 16 + 2 * t, :] = sq[:H, :NP]
            ss[:, g * 16 + 2 * t + 1, :] = sq[:H, NP:]

    scale = DH**-0.5
    slot = iota((H, 32, NP), 1)
    real = (slot & 15) < VL
    inv = lax.rsqrt(ss[...] * (1.0 / DH) + 1e-6)
    s0 = scale * inv * sn[...]
    s = jnp.where(real, s0 + bi[...], -1e30)
    m = jnp.max(s, axis=1, keepdims=True)
    e = jnp.where(real, jnp.exp(s - m), 0.0)
    at[...] = e
    ml_buf[i, 0] = m[:, 0, :]
    ml_buf[i, 1] = jnp.sum(e, axis=1)
    mls = [
        remote(ml_buf.at[i], ml_buf.at[i], ml_ss.at[t - 1], ml_rs.at[t - 1], var=(i + t) % 8)
        for t in range(1, 8)
    ]
    for cp in mls:
        cp.start()
    sn[...] = s0
    ss[...] = inv

    for cp in gsends:
        cp.wait()
    o = iota((NP, NP), 0)
    src = (o & 7) * 16 + (o >> 4) * 2 + ((o >> 3) & 1)
    perm = jnp.where(src == iota((NP, NP), 1), 1.0, 0.0).astype(bf16)
    gcf = dot(perm, g_buf[...].reshape(NP, D))
    gc[...] = gcf.astype(bf16)
    gct = gcf.T
    top_half = iota((NP, NP), 0) < DH
    for pair in range(4):
        piece = gct[pair * 128 : (pair + 1) * 128]
        blocks = jnp.concatenate(
            [jnp.where(top_half, piece, 0.0), jnp.where(top_half, 0.0, piece)], axis=1
        ).astype(bf16)
        for g in range(2):
            prod = dot(wev[g * GR : (g + 1) * GR, pair * 128 : (pair + 1) * 128], blocks)
            fg_rows = ff[g]
            hi, lo = split(prod * jnp.concatenate([fg_rows, fg_rows], axis=1))
            got = dot(sums, hi) + dot(sums, lo)
            ga[2 * pair, g * 16 : (g + 1) * 16, :] = got[:, :NP]
            ga[2 * pair + 1, g * 16 : (g + 1) * 16, :] = got[:, NP:]
    r_buf[i] = jnp.sum(at[...] * ga[...], axis=1)
    rss = [
        remote(r_buf.at[i], r_buf.at[i], r_ss.at[t - 1], r_rs.at[t - 1], var=(i + t) % 8)
        for t in range(1, 8)
    ]
    for cp in rss:
        cp.start()
    for cp in mls:
        cp.wait()
    mall = ml_buf[0, 0]
    for n in range(1, 8):
        mall = jnp.maximum(mall, ml_buf[n, 0])
    lall = jnp.zeros((H, NP), f32)
    for n in range(8):
        lall = lall + jnp.exp(ml_buf[n, 0] - mall) * ml_buf[n, 1]
    mine = jnp.exp(ml_buf[i, 0] - mall) / lall
    at[...] = at[...] * mine[:, None, :]

    def times_fields(ref, h, g):
        x = ref[h, g * 16 : (g + 1) * 16, :]
        parts = [jnp.broadcast_to(x[v : v + 1], (PIX, NP)) for v in range(VL)] + [x]
        return (jnp.concatenate(parts, axis=0) * ff[g]).astype(bf16)

    def put(buf, x):
        buf[:D, :] = x[:, : D // 2]
        buf[D:, :] = x[:, D // 2 :]

    sib = y * 2 + 1 - c

    def core_sum_start(buf, r1, s_sem, r_sem):
        cp = remote(buf.at[pl.ds((1 - c) * D, D)], r1, s_sem.at[0], r_sem.at[0], patch=sib)
        cp.start()
        return cp

    def at16(w):
        return dict(var=(w // 4) * 2 + xh, patch=(w % 4) * 2 + c)

    def core_sum_end(cp, buf, r1, s1, r2, s_sem, r_sem):
        cp.wait()
        s1[...] = (buf[pl.ds(c * D, D), :].astype(f32) + r1[...].astype(f32)).astype(bf16)
        cps = []
        for t in range(1, 16):
            w = (w_me + t) % 16
            cps.append(remote(s1.at[pl.ds(w * 32, 32)], r2.at[t - 1], s_sem.at[t], r_sem.at[t], **at16(w)))
        for cp in cps:
            cp.start()
        return cps

    def zy_sum_end(cps, s1, r2, s2, r3, s_sem, r_sem):
        for cp in cps:
            cp.wait()
        tot = s1[pl.ds(w_me * 32, 32), :].astype(f32)
        for n in range(15):
            tot = tot + r2[n].astype(f32)
        s2[...] = tot.astype(bf16)
        cp = remote(s2, r3, s_sem.at[16], r_sem.at[16], var=z * 2 + 1 - xh)
        cp.start()
        return cp

    def x_sum_end(cp, s2, r3, fin, s_sem, r_sem):
        cp.wait()
        row = c * D + w_me * 32
        fin[pl.ds(row, 32), :] = (s2[...].astype(f32) + r3[...].astype(f32)).astype(bf16)
        rows = fin.at[pl.ds(row, 32)]
        cps = []
        for t in range(1, 16):
            cps.append(remote(rows, rows, s_sem.at[16 + t], r_sem.at[16 + t], **at16((w_me + t) % 16)))
        for cp in cps:
            cp.start()
        return cps

    def gather_end(cps, fin, s_sem, r_sem):
        for cp in cps:
            cp.wait()
        half = fin.at[pl.ds(c * D, D)]
        cp = remote(half, half, s_sem.at[32], r_sem.at[32], patch=sib)
        cp.start()
        return cp

    low = iota((NP, 128), 1) < DH
    lowg = iota((GR, 128), 1) < DH
    zero = jnp.zeros((), bf16)
    for pair in range(4):
        lanes = slice(pair * 128, (pair + 1) * 128)
        piece = gc[:, lanes].astype(f32)
        gd = jnp.concatenate([jnp.where(low, piece, 0.0), jnp.where(low, 0.0, piece)], axis=0)
        gd = gd.astype(bf16)
        for g in range(2):
            pieces = []
            for n in range(2):
                x = times_fields(at, 2 * pair + n, g)
                eb[2 * pair + n, g * GR : (g + 1) * GR, :] = x
                pieces.append(x)
            fg[g * GR : (g + 1) * GR, D + pair * 128 : D + (pair + 1) * 128] = dot(
                jnp.concatenate(pieces, axis=1), gd
            ).astype(bf16)
    put(vb, dot(wat[...], fg[:, D:]).astype(bf16))
    v1 = core_sum_start(vb, vr1, v_ss, v_rs)

    for h in range(H):
        acc = dot(wevt[0, h * DH : (h + 1) * DH, :], eb[h, :GR, :])
        acc = acc + dot(wevt[1, h * DH : (h + 1) * DH, :], eb[h, GR:, :])
        ctxt[h * DH : (h + 1) * DH, :] = acc
    c_snd[...] = ctxt[...].T.astype(bf16).reshape(8, 16, D)
    cs = []
    for t in range(1, 8):
        peer = (i + t) % 8
        cs.append(remote(c_snd.at[peer], c_buf.at[i], c_ss.at[t - 1], c_rs.at[t - 1], var=peer))
    v2 = core_sum_end(v1, vb, vr1, vs1, vr2, v_ss, v_rs)
    for cp in cs:
        cp.start()
    c_buf[i] = c_snd[i]

    for cp in rss:
        cp.wait()
    rall = jnp.zeros((H, NP), f32)
    for n in range(8):
        rall = rall + jnp.exp(ml_buf[n, 0] - mall) * r_buf[n]
    rall = rall / lall
    inv = ss[...]
    gs = at[...] * (ga[...] - rall[:, None, :])
    ca[...] = scale * inv * gs
    cb[...] = (-1.0 / DH) * inv * inv * gs * sn[...]

    same = var_of(iota((GR, GR), 0)) == var_of(iota((GR, GR), 1))
    for pair in range(4):
        lanes = slice(pair * 128, (pair + 1) * 128)
        qp = jnp.broadcast_to(qrow[:, lanes], (NP, 128))
        qd = jnp.concatenate([jnp.where(low, qp, 0.0), jnp.where(low, 0.0, qp)], axis=0).astype(bf16)
        for g in range(2):
            wp = wek[g * GR : (g + 1) * GR, lanes].astype(f32)
            wd = jnp.concatenate([jnp.where(lowg, wp, 0.0), jnp.where(lowg, 0.0, wp)], axis=0)
            wd = wd.astype(bf16)
            af, ms = [], []
            for n in range(2):
                af.append(times_fields(ca, 2 * pair + n, g))
                mm = dot(times_fields(cb, 2 * pair + n, g), fb[g], NT)
                ms.append(jnp.where(same, mm, 0.0).astype(bf16))
            total = dot(jnp.concatenate(af, axis=1), qd) + dot(jnp.concatenate(ms, axis=1), wd)
            fg[g * GR : (g + 1) * GR, lanes] = total.astype(bf16)
    put(kb, dot(wat[...], fg[:, :D]).astype(bf16))
    k1 = core_sum_start(kb, kr1, k_ss, k_rs)
    for g in range(2):
        rows = slice(g * GR, (g + 1) * GR)
        egb[rows, :] = (dot(fg[rows, :D], wk[...], NT) + dot(fg[rows, D:], wv[...], NT)).astype(bf16)
    ex1 = remote(egb.at[pl.ds((1 - c) * GR, GR)], re1, e_ss.at[0], e_rs.at[0], patch=sib)
    ex1.start()

    k2 = core_sum_end(k1, kb, kr1, ks1, kr2, k_ss, k_rs)
    ex1.wait()
    e1[...] = (egb[pl.ds(c * GR, GR), :].astype(f32) + re1[...].astype(f32)).astype(bf16)
    ex2 = []
    for t in range(1, 4):
        peer = (y + t) % 4
        ex2.append(
            remote(e1.at[pl.ds(peer * 64, 64)], re2.at[t - 1], e_ss.at[t], e_rs.at[t], patch=peer * 2 + c)
        )
    for cp in ex2:
        cp.start()

    for cp in cs:
        cp.wait()
    cx = c_buf[0].astype(f32)
    for n in range(1, 8):
        cx = cx + c_buf[n].astype(f32)
    row = off_s[0] + 2 * j + (iota((16, 180), 0) >> 3)
    hot = jnp.where(row == iota((16, 180), 1), 1.0, 0.0).astype(bf16)
    agg = (dot(cx.astype(bf16), wo[...]) + dot(hot, lat_v[...])).astype(bf16)
    dst = iota((NP, 16), 0)
    r = (dst & 15) - 2 * j
    take = ((r >= 0) & (r < 2)) & (iota((NP, 16), 1) == r * 8 + (dst >> 4))
    a_snd[...] = dot(jnp.where(take, 1.0, 0.0).astype(bf16), agg).astype(bf16).reshape(8, 16, D)
    sends = []
    for t in range(1, 8):
        peer = (j + t) % 8
        sends.append(remote(a_snd.at[peer], a_buf.at[j], a_ss.at[t - 1], a_rs.at[t - 1], patch=peer))
    for cp in sends:
        cp.start()
    a_buf[j] = a_snd[j]

    v3 = zy_sum_end(v2, vs1, vr2, vs2, vr3, v_ss, v_rs)
    for cp in ex2:
        cp.wait()
    tot = e1[pl.ds(y * 64, 64), :].astype(f32)
    for n in range(3):
        tot = tot + re2[n].astype(f32)
    erow = c * GR + y * 64
    fine[pl.ds(erow, 64), :] = tot.astype(bf16)
    ex3 = []
    for t in range(1, 4):
        peer = (y + t) % 4
        own_rows = fine.at[pl.ds(erow, 64)]
        ex3.append(remote(own_rows, own_rows, e_ss.at[3 + t], e_rs.at[3 + t], patch=peer * 2 + c))
    for cp in ex3:
        cp.start()
    v4 = x_sum_end(v3, vs2, vr3, vfin, v_ss, v_rs)
    k3 = zy_sum_end(k2, ks1, kr2, ks2, kr3, k_ss, k_rs)
    for cp in ex3:
        cp.wait()
    half = fine.at[pl.ds(c * GR, GR)]
    ex4 = remote(half, half, e_ss.at[7], e_rs.at[7], patch=sib)
    ex4.start()
    k4 = x_sum_end(k3, ks2, kr3, kfin, k_ss, k_rs)

    for cp in sends:
        cp.wait()
    acc = a_buf[0].astype(f32)
    for n in range(1, 8):
        acc = acc + a_buf[n].astype(f32)
    a_snd[0] = acc.astype(bf16)
    outs = [pltpu.make_async_copy(a_snd.at[0], agg_o, lsem.at[13])]
    outs[0].start()
    ex4.wait()
    outs.append(pltpu.make_async_copy(fine, eg_o, lsem.at[14]))
    outs[1].start()
    v5 = gather_end(v4, vfin, v_ss, v_rs)
    v5.wait()
    outs.append(pltpu.make_async_copy(vfin, vg_o, lsem.at[15]))
    outs[2].start()
    k5 = gather_end(k4, kfin, k_ss, k_rs)
    k5.wait()
    outs.append(pltpu.make_async_copy(kfin, kg_o, lsem.at[16]))
    outs[3].start()
    for cp in outs:
        cp.wait()


def cast_kernel(agg_h, eg_h, kg_h, vg_h, agg_o, emb_o, var_o, kg_o, vg_o, agg, eg, kg, vg, emb, var, kgf, vgf, sem):
    def copy(n, src, dst):
        cp = pltpu.make_async_copy(src, dst, sem.at[n])
        cp.start()
        return cp

    first = [copy(0, vg_h, vg), copy(1, kg_h, kg), copy(2, eg_h, eg), copy(3, agg_h, agg)]
    outs = []
    for n, (src, full, dst) in enumerate(((vg, vgf, vg_o), (kg, kgf, kg_o))):
        first[n].wait()
        full[:, : D // 2] = src[:D].astype(f32)
        full[:, D // 2 :] = src[D:].astype(f32)
        outs.append(copy(4 + n, full, dst))
    first[2].wait()
    for g in range(2):
        emb[g * VL : (g + 1) * VL] = eg[g * GR : g * GR + VL * PIX].astype(f32).reshape(VL, PIX, D)
        var[g * VL : (g + 1) * VL] = eg[g * GR + VL * PIX : (g + 1) * GR].astype(f32)[:VL]
    outs += [copy(6, emb, emb_o), copy(7, var, var_o)]
    first[3].wait()
    outs.append(copy(8, agg, agg_o))
    for cp in outs:
        cp.wait()


def local(fields, var_ids, level_of, window_offset, w_embed, var_emb, w_key, w_value, w_out,
          latent_query, bias_table, lat_emb, d_aggregated):
    hbm = pl.BlockSpec(memory_space=pltpu.HBM)
    dma = pltpu.SemaphoreType.DMA

    def v(*shape, dtype=bf16):
        return pltpu.VMEM(shape, dtype)

    scratch = [
        pltpu.SMEM((240,), i32), pltpu.SMEM((240,), i32), pltpu.SMEM((1,), i32), pltpu.SMEM((H, 38), f32),
        v(H, DH, dtype=f32), v(180, D), v(NV, 2, 1024), v(240, PIX, D), v(256, D), v(D, D), v(D, D), v(D, D), dma((17,)),
        v(8, 16, D), dma((7,)), dma((7,)),
        v(8, 16, D), v(8, 16, D), dma((7,)), dma((7,)),
        v(8, 2, H, NP, dtype=f32), dma((7,)), dma((7,)),
        v(8, H, NP, dtype=f32), dma((7,)), dma((7,)),
        v(8, 16, D), v(8, 16, D), dma((7,)), dma((7,)),
        v(8, 16, D), v(8, 16, D), dma((7,)), dma((7,)),
        v(2 * D, D // 2), v(D, D // 2), v(15, 32, D // 2), v(32, D // 2), v(D, D // 2), v(32, D // 2), v(2 * D, D // 2),
        v(2 * D, D // 2), v(D, D // 2), v(15, 32, D // 2), v(32, D // 2), v(D, D // 2), v(32, D // 2), v(2 * D, D // 2),
        v(D, D), v(GR, D), v(3, 64, D), v(GR, D), v(D, D),
        dma((33,)), dma((33,)), dma((33,)), dma((33,)), dma((8,)), dma((8,)),
        v(D, D), v(D, D), v(D, D), v(D, D), v(2, D, GR), v(2, D, GR),
        v(2, GR, NP, dtype=f32), v(2, GR, NP),
    ]
    scratch += [v(H, 32, NP, dtype=f32)] * 4 + [v(NP, D)] + [v(H, 32, NP, dtype=f32)] * 3
    scratch += [v(H, D, NP), v(D, 2 * D), v(D, NP, dtype=f32)]
    agg, eg, kg, vg = pl.pallas_call(
        kernel,
        out_shape=[
            jax.ShapeDtypeStruct((16, D), bf16),
            jax.ShapeDtypeStruct((D, D), bf16),
            jax.ShapeDtypeStruct((2 * D, D // 2), bf16),
            jax.ShapeDtypeStruct((2 * D, D // 2), bf16),
        ],
        in_specs=[hbm] * 13,
        out_specs=[hbm] * 4,
        scratch_shapes=scratch,
        compiler_params=pltpu.CompilerParams(
            collective_id=0, has_side_effects=True, vmem_limit_bytes=62 * 1024 * 1024
        ),
    )(
        var_ids, level_of, window_offset, bias_table.T,
        fields, w_embed, var_emb, w_key, w_value, w_out, latent_query, lat_emb,
        d_aggregated.reshape(16, D),
    )
    agg, embed, var, key_grad, value_grad = pl.pallas_call(
        cast_kernel,
        out_shape=[
            jax.ShapeDtypeStruct((16, D), bf16),
            jax.ShapeDtypeStruct((NV, PIX, D), f32),
            jax.ShapeDtypeStruct((NV, D), f32),
            jax.ShapeDtypeStruct((D, D), f32),
            jax.ShapeDtypeStruct((D, D), f32),
        ],
        in_specs=[hbm] * 4,
        out_specs=[hbm] * 5,
        scratch_shapes=[
            v(16, D), v(D, D), v(2 * D, D // 2), v(2 * D, D // 2),
            v(NV, PIX, D, dtype=f32), v(NV, D, dtype=f32), v(D, D, dtype=f32), v(D, D, dtype=f32),
            dma((9,)),
        ],
        compiler_params=pltpu.CompilerParams(vmem_limit_bytes=62 * 1024 * 1024),
    )(agg, eg, kg, vg)
    return agg.reshape(16, 1, D), embed, var, key_grad, value_grad


def solution(mesh):
    split_rows = P(("win", "var"), "patch", None)
    column = P("win", ("var", "patch"), None)
    in_specs = (split_rows, P(), P(), P("win")) + (P(),) * 8 + (column,)
    out_specs = (
        column,
        P(("win", "var"), None, None),
        P(("win", "var"), None),
        P("win", None),
        P("win", None),
    )
    return jax.shard_map(local, mesh=mesh, in_specs=in_specs, out_specs=out_specs, check_vma=False)
```

```python
import jax
import jax.numpy as jnp
from jax import lax
from jax.experimental import pallas as pl
from jax.experimental.pallas import tpu as pltpu
from jax.sharding import PartitionSpec as P

f32, bf16, i32 = jnp.float32, jnp.bfloat16, jnp.int32
NV, VL, PIX, D, H, DH, NP = 30, 15, 16, 512, 8, 64, 128
GR = 256
NN = (((1,), (0,)), ((), ()))
NT = (((1,), (1,)), ((), ()))


def iota(shape, dim):
    return lax.broadcasted_iota(i32, shape, dim)


def dot(a, b, dims=NN):
    return lax.dot_general(a, b, dims, preferred_element_type=f32)


def split(x):
    hi = x.astype(bf16)
    return hi, (x - hi.astype(f32)).astype(bf16)


def hops(d):
    return min(d, 4 - d)


VAR = sorted(((a, b) for a in range(4) for b in range(2)), key=lambda o: -hops(o[0]) - 2 * o[1])[:-1]
PATCH = sorted(((a, b) for a in range(4) for b in range(2)), key=lambda o: -hops(o[0]) - o[1] / 4)[:-1]
SQUARE = sorted(((a, b) for a in range(4) for b in range(4)), key=lambda o: -hops(o[0]) - hops(o[1]))[:-1]


def var_of(row):
    return jnp.where(row < VL * PIX, row >> 4, row - VL * PIX)


def kernel(
    ids_h, lvl_h, off_h, bias_h,
    fields_h, we_h, ve_h, wk_h, wv_h, wo_h, q_h, lat_h, d_h,
    agg_o, eg_o, kg_o, vg_o,
    ids_s, lvl_s, off_s, bias_s, q_v, lat_v, fld, wem, vem, wk, wv, wo, lsem,
    x_buf, x_ss, x_rs,
    g_snd, g_buf, g_ss, g_rs,
    ml_buf, ml_ss, ml_rs,
    r_buf, r_ss, r_rs,
    c_snd, c_buf, c_ss, c_rs,
    a_snd, a_buf, a_ss, a_rs,
    kb, kr1, kr2, kr3, ks1, ks2, kfin,
    vb, vr1, vr2, vr3, vs1, vs2, vfin,
    egb, re1, re2, e1, fine,
    k_ss, k_rs, v_ss, v_rs, e_ss, e_rs,
    wa, wat, wot, wek, wev, wekt, wevt, ff, fb, bi, ss, sn, ga, gc, at, ca, cb, eb, fg, ctxt,
):
    i, j = lax.axis_index("var"), lax.axis_index("patch")
    z, xh = i // 2, i % 2
    y, c = j // 2, j % 2
    w_me = z * 4 + y
    var_peers = [((z + a) % 4) * 2 + (xh + b) % 2 for a, b in VAR]
    patch_peers = [((y + a) % 4) * 2 + (c + b) % 2 for a, b in PATCH]
    square_peers = [((z + a) % 4, (y + b) % 4) for a, b in SQUARE]

    pending = []

    class Tr:
        def __init__(self, cp):
            self.cp = cp

        def start(self):
            self.cp.start()
            pending.append(self)

        def wait(self):
            self.cp.wait()
            pending.remove(self)

    def remote(src, dst, ssem, rsem, **dev):
        return Tr(pltpu.make_async_remote_copy(
            src_ref=src,
            dst_ref=dst,
            send_sem=ssem,
            recv_sem=rsem,
            device_id=dev,
            device_id_type=pl.DeviceIdType.MESH,
        ))

    local = [
        Tr(pltpu.make_async_copy(src, dst, lsem.at[n]))
        for n, (src, dst) in enumerate(
            [
                (fields_h, fld),
                (we_h, wem),
                (ve_h, vem.at[pl.ds(0, 240)]),
                (wk_h, wk),
                (wv_h, wv),
                (wo_h, wo),
                (d_h, x_buf.at[i]),
                (ids_h, ids_s),
                (lvl_h, lvl_s),
                (off_h, off_s),
                (bias_h, bias_s),
                (q_h, q_v),
                (lat_h, lat_v),
            ]
        )
    ]
    for cp in local:
        cp.start()

    barrier = pltpu.get_barrier_semaphore()
    peers = [dict(var=a * 2 + xh, patch=b * 2 + c) for (a, b), (d, e) in zip(square_peers, SQUARE) if d and e]
    peers += [dict(var=n) for n in var_peers] + [dict(patch=n) for n in patch_peers]
    for dev in peers:
        pl.semaphore_signal(barrier, inc=1, device_id=dev, device_id_type=pl.DeviceIdType.MESH)

    for n in range(7, 13):
        local[n].wait()
    def bias_step(v, _):
        lvl = lvl_s[ids_s[i * NV + v]]
        slot = v + v // VL
        for h in range(H):
            bi[h, pl.ds(slot, 1), :] = jnp.full((1, NP), bias_s[h, lvl], f32)
        return 0

    lax.fori_loop(0, NV, bias_step, 0)

    local[0].wait()
    lane_col = iota((8, NP), 1) >> 4
    own = lane_col == iota((8, NP), 0)
    pick = ((iota((PIX, NP), 1) & 15) == iota((PIX, NP), 0)).astype(bf16)
    for g in range(2):
        parts = []
        for v in range(VL):
            row = fld[g * VL + v].astype(f32)
            for b in range(8):
                for r in range(2):
                    piece = jnp.broadcast_to(row[r : r + 1, b * 128 : (b + 1) * 128], (8, 128))
                    parts.append(jnp.where(own, piece, 0.0))
        spread = jnp.concatenate(parts, axis=0).astype(bf16)
        ft = dot(pick, spread, NT)
        for v in range(VL):
            ff[g, v * PIX : (v + 1) * PIX, :] = ft[:, v * NP : (v + 1) * NP]
        ff[g, VL * PIX :, :] = jnp.where(iota((16, NP), 0) < VL, 1.0, 0.0)
        fb[g] = ff[g].astype(bf16)

    pl.semaphore_wait(barrier, len(peers))
    xs = [remote(d_h, x_buf.at[i], x_ss.at[n], x_rs.at[n], var=peer) for n, peer in enumerate(var_peers)]
    for cp in xs:
        cp.start()

    local[1].wait()

    def gather_step(v, _):
        g = v // VL
        row = pl.multiple_of(g * GR + (v - g * VL) * PIX, PIX)
        wa[pl.ds(row, PIX), :] = wem[ids_s[i * NV + v]]
        return 0

    lax.fori_loop(0, NV, gather_step, 0)
    vem[240:, :] = jnp.zeros((16, D), bf16)
    local[2].wait()
    for g in range(2):
        want = jnp.full((16, 256), -1, i32)
        for v in range(VL):
            want = jnp.where(iota((16, 256), 0) == v, ids_s[i * NV + g * VL + v], want)
        hot = jnp.where(want == iota((16, 256), 1), 1.0, 0.0).astype(bf16)
        wa[g * GR + VL * PIX : (g + 1) * GR, :] = dot(hot, vem[...]).astype(bf16)
    local[3].wait()
    local[4].wait()
    wat[...] = wa[...].T
    local[5].wait()
    wot[...] = wo[...].T
    wek[...] = dot(wa[...], wk[...]).astype(bf16)
    wev[...] = dot(wa[...], wv[...]).astype(bf16)
    for g in range(2):
        wekt[g] = wek[g * GR : (g + 1) * GR, :].T
        wevt[g] = wev[g * GR : (g + 1) * GR, :].T

    spread_q = jnp.where((iota((DH, D), 1) & 63) == iota((DH, D), 0), 1.0, 0.0)
    qall = jnp.dot(q_v[...], spread_q, precision=lax.Precision.HIGHEST, preferred_element_type=f32)
    qblk = jnp.where((iota((H, D), 1) >> 6) == iota((H, D), 0), qall, 0.0)
    qrow = jnp.sum(qblk, axis=0, keepdims=True)
    wq = dot(jnp.concatenate(split(qblk), axis=0), wk[...], NT)
    wq = wq[:H] + wq[H:]
    aq = dot(jnp.concatenate(split(wq), axis=0), wa[...], NT)
    aq = aq[:H] + aq[H:]
    lane_var = var_of(iota((16, GR), 1))
    member = lane_var == iota((16, GR), 0)
    sums = jnp.where(member, 1.0, 0.0).astype(bf16)
    for g in range(2):
        rows = [
            jnp.where(member, jnp.broadcast_to(aq[h : h + 1, g * GR : (g + 1) * GR], (16, GR)), 0.0)
            for h in range(H)
        ]
        hi, lo = split(jnp.concatenate(rows, axis=0))
        got = dot(hi, fb[g]) + dot(lo, fb[g])
        for h in range(H):
            sn[h, g * 16 : (g + 1) * 16, :] = got[h * 16 : (h + 1) * 16]

    heads = jnp.where((iota((16, D), 1) >> 6) == iota((16, D), 0), 1.0, 0.0).astype(bf16)
    tile_row = iota((16, NP), 0)
    def square_sums(g):
        ones = ff[g, VL * PIX :, :]
        for t in range(8):
            cols = []
            for v in (2 * t, 2 * t + 1):
                top = []
                if v < VL:
                    if v > 0:
                        top.append(jnp.zeros((v * PIX, NP), bf16))
                    top.append(fb[g, v * PIX : (v + 1) * PIX, :])
                    if v < VL - 1:
                        top.append(jnp.zeros(((VL - 1 - v) * PIX, NP), bf16))
                else:
                    top.append(jnp.zeros((VL * PIX, NP), bf16))
                top.append(jnp.where(tile_row == v, ones, 0.0).astype(bf16))
                cols.append(jnp.concatenate(top, axis=0))
            keys = dot(wekt[g], jnp.concatenate(cols, axis=1))
            sq = dot(heads, (keys * keys).astype(bf16))
            ss[:, g * 16 + 2 * t, :] = sq[:H, :NP]
            ss[:, g * 16 + 2 * t + 1, :] = sq[:H, NP:]


    square_sums(0)

    local[6].wait()
    for cp in xs:
        cp.wait()
    gx = dot(x_buf[...].reshape(NP, D), wot[...]).astype(bf16)
    o = iota((NP, NP), 0)
    src = ((o >> 1) & 7) * 16 + (o >> 4) * 2 + (o & 1)
    perm = jnp.where(src == iota((NP, NP), 1), 1.0, 0.0).astype(bf16)
    gs_rows = dot(perm, gx).astype(bf16)
    g_snd[...] = gs_rows.reshape(8, 16, D)
    gsends = []
    for n, peer in enumerate(patch_peers):
        gsends.append(remote(g_snd.at[peer], g_buf.at[j], g_ss.at[n], g_rs.at[n], patch=peer))
    for cp in gsends:
        cp.start()
    g_buf[j] = g_snd[j]

    square_sums(1)
    scale = DH**-0.5
    slot = iota((H, 32, NP), 1)
    real = (slot & 15) < VL
    inv = lax.rsqrt(ss[...] * (1.0 / DH) + 1e-6)
    s0 = scale * inv * sn[...]
    s = jnp.where(real, s0 + bi[...], -1e30)
    m = jnp.max(s, axis=1, keepdims=True)
    e = jnp.where(real, jnp.exp(s - m), 0.0)
    at[...] = e
    ml_buf[i, 0] = m[:, 0, :]
    ml_buf[i, 1] = jnp.sum(e, axis=1)
    mls = [
        remote(ml_buf.at[i], ml_buf.at[i], ml_ss.at[n], ml_rs.at[n], var=peer)
        for n, peer in enumerate(var_peers)
    ]
    for cp in mls:
        cp.start()
    sn[...] = s0
    ss[...] = inv

    for cp in gsends:
        cp.wait()
    o = iota((NP, NP), 0)
    src = (o & 7) * 16 + (o >> 4) * 2 + ((o >> 3) & 1)
    perm = jnp.where(src == iota((NP, NP), 1), 1.0, 0.0).astype(bf16)
    gcf = dot(perm, g_buf[...].reshape(NP, D))
    gc[...] = gcf.astype(bf16)
    gct = gcf.T
    top_half = iota((NP, NP), 0) < DH
    for pair in range(4):
        piece = gct[pair * 128 : (pair + 1) * 128]
        blocks = jnp.concatenate(
            [jnp.where(top_half, piece, 0.0), jnp.where(top_half, 0.0, piece)], axis=1
        ).astype(bf16)
        for g in range(2):
            prod = dot(wev[g * GR : (g + 1) * GR, pair * 128 : (pair + 1) * 128], blocks)
            fg_rows = ff[g]
            hi, lo = split(prod * jnp.concatenate([fg_rows, fg_rows], axis=1))
            got = dot(sums, hi) + dot(sums, lo)
            ga[2 * pair, g * 16 : (g + 1) * 16, :] = got[:, :NP]
            ga[2 * pair + 1, g * 16 : (g + 1) * 16, :] = got[:, NP:]
    r_buf[i] = jnp.sum(at[...] * ga[...], axis=1)
    rss = [
        remote(r_buf.at[i], r_buf.at[i], r_ss.at[n], r_rs.at[n], var=peer)
        for n, peer in enumerate(var_peers)
    ]
    for cp in rss:
        cp.start()
    for cp in mls:
        cp.wait()
    mall = ml_buf[0, 0]
    for n in range(1, 8):
        mall = jnp.maximum(mall, ml_buf[n, 0])
    lall = jnp.zeros((H, NP), f32)
    for n in range(8):
        lall = lall + jnp.exp(ml_buf[n, 0] - mall) * ml_buf[n, 1]
    mine = jnp.exp(ml_buf[i, 0] - mall) / lall
    at[...] = at[...] * mine[:, None, :]

    def times_fields(ref, h, g):
        x = ref[h, g * 16 : (g + 1) * 16, :]
        parts = [jnp.broadcast_to(x[v : v + 1], (PIX, NP)) for v in range(VL)] + [x]
        return (jnp.concatenate(parts, axis=0) * ff[g]).astype(bf16)

    def put(buf, x):
        buf[:D, :] = x[:, : D // 2]
        buf[D:, :] = x[:, D // 2 :]

    sib = y * 2 + 1 - c

    def core_sum_start(buf, r1, s_sem, r_sem):
        cp = remote(buf.at[pl.ds((1 - c) * D, D)], r1, s_sem.at[0], r_sem.at[0], patch=sib)
        cp.start()
        return cp

    def core_sum_end(cp, buf, r1, s1, r2, s_sem, r_sem):
        cp.wait()
        s1[...] = (buf[pl.ds(c * D, D), :].astype(f32) + r1[...].astype(f32)).astype(bf16)
        cps = []
        for n, (a, b) in enumerate(square_peers):
            part = s1.at[pl.ds((a * 4 + b) * 32, 32)]
            cps.append(
                remote(part, r2.at[n], s_sem.at[n + 1], r_sem.at[n + 1], var=a * 2 + xh, patch=b * 2 + c)
            )
        for cp in cps:
            cp.start()
        return cps

    def zy_sum_end(cps, s1, r2, s2, r3, s_sem, r_sem):
        for cp in cps:
            cp.wait()
        tot = s1[pl.ds(w_me * 32, 32), :].astype(f32)
        for n in range(15):
            tot = tot + r2[n].astype(f32)
        s2[...] = tot.astype(bf16)
        cp = remote(s2, r3, s_sem.at[16], r_sem.at[16], var=z * 2 + 1 - xh)
        cp.start()
        return cp

    def x_sum_end(cp, s2, r3, fin, s_sem, r_sem):
        cp.wait()
        row = c * D + w_me * 32
        fin[pl.ds(row, 32), :] = (s2[...].astype(f32) + r3[...].astype(f32)).astype(bf16)
        rows = fin.at[pl.ds(row, 32)]
        cps = []
        for n, (a, b) in enumerate(square_peers):
            cps.append(
                remote(rows, rows, s_sem.at[17 + n], r_sem.at[17 + n], var=a * 2 + xh, patch=b * 2 + c)
            )
        for cp in cps:
            cp.start()
        return cps

    def gather_end(cps, fin, s_sem, r_sem):
        for cp in cps:
            cp.wait()
        half = fin.at[pl.ds(c * D, D)]
        cp = remote(half, half, s_sem.at[32], r_sem.at[32], patch=sib)
        cp.start()
        return cp

    low = iota((NP, 128), 1) < DH
    lowg = iota((GR, 128), 1) < DH
    zero = jnp.zeros((), bf16)
    for pair in range(4):
        lanes = slice(pair * 128, (pair + 1) * 128)
        piece = gc[:, lanes].astype(f32)
        gd = jnp.concatenate([jnp.where(low, piece, 0.0), jnp.where(low, 0.0, piece)], axis=0)
        gd = gd.astype(bf16)
        for g in range(2):
            pieces = []
            for n in range(2):
                x = times_fields(at, 2 * pair + n, g)
                eb[2 * pair + n, g * GR : (g + 1) * GR, :] = x
                pieces.append(x)
            fg[g * GR : (g + 1) * GR, D + pair * 128 : D + (pair + 1) * 128] = dot(
                jnp.concatenate(pieces, axis=1), gd
            ).astype(bf16)
    put(vb, dot(wat[...], fg[:, D:]).astype(bf16))
    v1 = core_sum_start(vb, vr1, v_ss, v_rs)


    for cp in rss:
        cp.wait()
    rall = jnp.zeros((H, NP), f32)
    for n in range(8):
        rall = rall + jnp.exp(ml_buf[n, 0] - mall) * r_buf[n]
    rall = rall / lall
    inv = ss[...]
    gs = at[...] * (ga[...] - rall[:, None, :])
    ca[...] = scale * inv * gs
    cb[...] = (-1.0 / DH) * inv * inv * gs * sn[...]

    same = var_of(iota((GR, GR), 0)) == var_of(iota((GR, GR), 1))
    for pair in range(4):
        lanes = slice(pair * 128, (pair + 1) * 128)
        qp = jnp.broadcast_to(qrow[:, lanes], (NP, 128))
        qd = jnp.concatenate([jnp.where(low, qp, 0.0), jnp.where(low, 0.0, qp)], axis=0).astype(bf16)
        for g in range(2):
            wp = wek[g * GR : (g + 1) * GR, lanes].astype(f32)
            wd = jnp.concatenate([jnp.where(lowg, wp, 0.0), jnp.where(lowg, 0.0, wp)], axis=0)
            wd = wd.astype(bf16)
            af, ms = [], []
            for n in range(2):
                af.append(times_fields(ca, 2 * pair + n, g))
                mm = dot(times_fields(cb, 2 * pair + n, g), fb[g], NT)
                ms.append(jnp.where(same, mm, 0.0).astype(bf16))
            total = dot(jnp.concatenate(af, axis=1), qd) + dot(jnp.concatenate(ms, axis=1), wd)
            fg[g * GR : (g + 1) * GR, lanes] = total.astype(bf16)
    put(kb, dot(wat[...], fg[:, :D]).astype(bf16))
    k1 = core_sum_start(kb, kr1, k_ss, k_rs)
    v2 = core_sum_end(v1, vb, vr1, vs1, vr2, v_ss, v_rs)
    k2 = core_sum_end(k1, kb, kr1, ks1, kr2, k_ss, k_rs)
    for g in range(2):
        rows = slice(g * GR, (g + 1) * GR)
        egb[rows, :] = (dot(fg[rows, :D], wk[...], NT) + dot(fg[rows, D:], wv[...], NT)).astype(bf16)
    ex1 = remote(egb.at[pl.ds((1 - c) * GR, GR)], re1, e_ss.at[0], e_rs.at[0], patch=sib)
    ex1.start()

    for h in range(H):
        acc = dot(wevt[0, h * DH : (h + 1) * DH, :], eb[h, :GR, :])
        acc = acc + dot(wevt[1, h * DH : (h + 1) * DH, :], eb[h, GR:, :])
        ctxt[h * DH : (h + 1) * DH, :] = acc
    c_snd[...] = ctxt[...].T.astype(bf16).reshape(8, 16, D)
    cs = []
    for n, peer in enumerate(var_peers):
        cs.append(remote(c_snd.at[peer], c_buf.at[i], c_ss.at[n], c_rs.at[n], var=peer))
    for cp in cs:
        cp.start()
    c_buf[i] = c_snd[i]

    ex1.wait()
    e1[...] = (egb[pl.ds(c * GR, GR), :].astype(f32) + re1[...].astype(f32)).astype(bf16)
    ex2 = []
    for t in range(1, 4):
        peer = (y + t) % 4
        ex2.append(
            remote(e1.at[pl.ds(peer * 64, 64)], re2.at[t - 1], e_ss.at[t], e_rs.at[t], patch=peer * 2 + c)
        )
    for cp in ex2:
        cp.start()

    v3 = zy_sum_end(v2, vs1, vr2, vs2, vr3, v_ss, v_rs)
    k3 = zy_sum_end(k2, ks1, kr2, ks2, kr3, k_ss, k_rs)
    v4 = x_sum_end(v3, vs2, vr3, vfin, v_ss, v_rs)
    for cp in ex2:
        cp.wait()
    tot = e1[pl.ds(y * 64, 64), :].astype(f32)
    for n in range(3):
        tot = tot + re2[n].astype(f32)
    erow = c * GR + y * 64
    fine[pl.ds(erow, 64), :] = tot.astype(bf16)
    ex3 = []
    for t in range(1, 4):
        peer = (y + t) % 4
        own_rows = fine.at[pl.ds(erow, 64)]
        ex3.append(remote(own_rows, own_rows, e_ss.at[3 + t], e_rs.at[3 + t], patch=peer * 2 + c))
    for cp in ex3:
        cp.start()
    k4 = x_sum_end(k3, ks2, kr3, kfin, k_ss, k_rs)
    for cp in cs:
        cp.wait()
    cx = c_buf[0].astype(f32)
    for n in range(1, 8):
        cx = cx + c_buf[n].astype(f32)
    row = off_s[0] + 2 * j + (iota((16, 180), 0) >> 3)
    hot = jnp.where(row == iota((16, 180), 1), 1.0, 0.0).astype(bf16)
    agg = (dot(cx.astype(bf16), wo[...]) + dot(hot, lat_v[...])).astype(bf16)
    dst = iota((NP, 16), 0)
    r = (dst & 15) - 2 * j
    take = ((r >= 0) & (r < 2)) & (iota((NP, 16), 1) == r * 8 + (dst >> 4))
    a_snd[...] = dot(jnp.where(take, 1.0, 0.0).astype(bf16), agg).astype(bf16).reshape(8, 16, D)
    sends = []
    for n, peer in enumerate(patch_peers):
        sends.append(remote(a_snd.at[peer], a_buf.at[j], a_ss.at[n], a_rs.at[n], patch=peer))
    for cp in sends:
        cp.start()
    a_buf[j] = a_snd[j]

    for cp in ex3:
        cp.wait()
    half = fine.at[pl.ds(c * GR, GR)]
    ex4 = remote(half, half, e_ss.at[7], e_rs.at[7], patch=sib)
    ex4.start()

    for cp in sends:
        cp.wait()
    acc = a_buf[0].astype(f32)
    for n in range(1, 8):
        acc = acc + a_buf[n].astype(f32)
    a_snd[0] = acc.astype(bf16)
    outs = [pltpu.make_async_copy(a_snd.at[0], agg_o, lsem.at[13])]
    outs[0].start()
    ex4.wait()
    outs.append(pltpu.make_async_copy(fine, eg_o, lsem.at[14]))
    outs[1].start()
    v5 = gather_end(v4, vfin, v_ss, v_rs)
    v5.wait()
    outs.append(pltpu.make_async_copy(vfin, vg_o, lsem.at[15]))
    outs[2].start()
    k5 = gather_end(k4, kfin, k_ss, k_rs)
    k5.wait()
    outs.append(pltpu.make_async_copy(kfin, kg_o, lsem.at[16]))
    outs[3].start()
    for cp in outs:
        cp.wait()


def cast_kernel(agg_h, eg_h, kg_h, vg_h, agg_o, emb_o, var_o, kg_o, vg_o, agg, eg, kg, vg, emb, var, kgf, vgf, sem):
    def copy(n, src, dst):
        cp = pltpu.make_async_copy(src, dst, sem.at[n])
        cp.start()
        return cp

    first = [copy(0, vg_h, vg), copy(1, kg_h, kg), copy(2, eg_h, eg), copy(3, agg_h, agg)]
    outs = []
    for n, (src, full, dst) in enumerate(((vg, vgf, vg_o), (kg, kgf, kg_o))):
        first[n].wait()
        full[:, : D // 2] = src[:D].astype(f32)
        full[:, D // 2 :] = src[D:].astype(f32)
        outs.append(copy(4 + n, full, dst))
    first[2].wait()
    for g in range(2):
        emb[g * VL : (g + 1) * VL] = eg[g * GR : g * GR + VL * PIX].astype(f32).reshape(VL, PIX, D)
        var[g * VL : (g + 1) * VL] = eg[g * GR + VL * PIX : (g + 1) * GR].astype(f32)[:VL]
    outs += [copy(6, emb, emb_o), copy(7, var, var_o)]
    first[3].wait()
    outs.append(copy(8, agg, agg_o))
    for cp in outs:
        cp.wait()


def local(fields, var_ids, level_of, window_offset, w_embed, var_emb, w_key, w_value, w_out,
          latent_query, bias_table, lat_emb, d_aggregated):
    hbm = pl.BlockSpec(memory_space=pltpu.HBM)
    dma = pltpu.SemaphoreType.DMA

    def v(*shape, dtype=bf16):
        return pltpu.VMEM(shape, dtype)

    scratch = [
        pltpu.SMEM((240,), i32), pltpu.SMEM((240,), i32), pltpu.SMEM((1,), i32), pltpu.SMEM((H, 38), f32),
        v(H, DH, dtype=f32), v(180, D), v(NV, 2, 1024), v(240, PIX, D), v(256, D), v(D, D), v(D, D), v(D, D), dma((17,)),
        v(8, 16, D), dma((7,)), dma((7,)),
        v(8, 16, D), v(8, 16, D), dma((7,)), dma((7,)),
        v(8, 2, H, NP, dtype=f32), dma((7,)), dma((7,)),
        v(8, H, NP, dtype=f32), dma((7,)), dma((7,)),
        v(8, 16, D), v(8, 16, D), dma((7,)), dma((7,)),
        v(8, 16, D), v(8, 16, D), dma((7,)), dma((7,)),
        v(2 * D, D // 2), v(D, D // 2), v(15, 32, D // 2), v(32, D // 2), v(D, D // 2), v(32, D // 2), v(2 * D, D // 2),
        v(2 * D, D // 2), v(D, D // 2), v(15, 32, D // 2), v(32, D // 2), v(D, D // 2), v(32, D // 2), v(2 * D, D // 2),
        v(D, D), v(GR, D), v(3, 64, D), v(GR, D), v(D, D),
        dma((33,)), dma((33,)), dma((33,)), dma((33,)), dma((8,)), dma((8,)),
        v(D, D), v(D, D), v(D, D), v(D, D), v(D, D), v(2, D, GR), v(2, D, GR),
        v(2, GR, NP, dtype=f32), v(2, GR, NP),
    ]
    scratch += [v(H, 32, NP, dtype=f32)] * 4 + [v(NP, D)] + [v(H, 32, NP, dtype=f32)] * 3
    scratch += [v(H, D, NP), v(D, 2 * D), v(D, NP, dtype=f32)]
    agg, eg, kg, vg = pl.pallas_call(
        kernel,
        out_shape=[
            jax.ShapeDtypeStruct((16, D), bf16),
            jax.ShapeDtypeStruct((D, D), bf16),
            jax.ShapeDtypeStruct((2 * D, D // 2), bf16),
            jax.ShapeDtypeStruct((2 * D, D // 2), bf16),
        ],
        in_specs=[hbm] * 13,
        out_specs=[hbm] * 4,
        scratch_shapes=scratch,
        compiler_params=pltpu.CompilerParams(
            collective_id=0, has_side_effects=True, vmem_limit_bytes=62 * 1024 * 1024
        ),
    )(
        var_ids, level_of, window_offset, bias_table.T,
        fields, w_embed, var_emb, w_key, w_value, w_out, latent_query, lat_emb,
        d_aggregated.reshape(16, D),
    )
    agg, embed, var, key_grad, value_grad = pl.pallas_call(
        cast_kernel,
        out_shape=[
            jax.ShapeDtypeStruct((16, D), bf16),
            jax.ShapeDtypeStruct((NV, PIX, D), f32),
            jax.ShapeDtypeStruct((NV, D), f32),
            jax.ShapeDtypeStruct((D, D), f32),
            jax.ShapeDtypeStruct((D, D), f32),
        ],
        in_specs=[hbm] * 4,
        out_specs=[hbm] * 5,
        scratch_shapes=[
            v(16, D), v(D, D), v(2 * D, D // 2), v(2 * D, D // 2),
            v(NV, PIX, D, dtype=f32), v(NV, D, dtype=f32), v(D, D, dtype=f32), v(D, D, dtype=f32),
            dma((9,)),
        ],
        compiler_params=pltpu.CompilerParams(vmem_limit_bytes=62 * 1024 * 1024),
    )(agg, eg, kg, vg)
    return agg.reshape(16, 1, D), embed, var, key_grad, value_grad


def solution(mesh):
    split_rows = P(("win", "var"), "patch", None)
    column = P("win", ("var", "patch"), None)
    in_specs = (split_rows, P(), P(), P("win")) + (P(),) * 8 + (column,)
    out_specs = (
        column,
        P(("win", "var"), None, None),
        P(("win", "var"), None),
        P("win", None),
        P("win", None),
    )
    return jax.shard_map(local, mesh=mesh, in_specs=in_specs, out_specs=out_specs, check_vma=False)
```

```python
import jax
import jax.numpy as jnp
from jax import lax
from jax.experimental import pallas as pl
from jax.experimental.pallas import tpu as pltpu
from jax.sharding import PartitionSpec as P

f32, bf16, i32 = jnp.float32, jnp.bfloat16, jnp.int32
NV, VL, PIX, D, H, DH, NP = 30, 15, 16, 512, 8, 64, 128
GR = 256
NN = (((1,), (0,)), ((), ()))
NT = (((1,), (1,)), ((), ()))


def iota(shape, dim):
    return lax.broadcasted_iota(i32, shape, dim)


def dot(a, b, dims=NN):
    return lax.dot_general(a, b, dims, preferred_element_type=f32)


def split(x):
    hi = x.astype(bf16)
    return hi, (x - hi.astype(f32)).astype(bf16)


def hops(d):
    return min(d, 4 - d)


VAR = sorted(((a, b) for a in range(4) for b in range(2)), key=lambda o: -hops(o[0]) - 2 * o[1])[:-1]
PATCH = sorted(((a, b) for a in range(4) for b in range(2)), key=lambda o: -hops(o[0]) - o[1] / 4)[:-1]
SQUARE = sorted(((a, b) for a in range(4) for b in range(4)), key=lambda o: -hops(o[0]) - hops(o[1]))[:-1]


def var_of(row):
    return jnp.where(row < VL * PIX, row >> 4, row - VL * PIX)


def kernel(
    ids_h, lvl_h, off_h, bias_h,
    fields_h, we_h, ve_h, wk_h, wv_h, wo_h, q_h, lat_h, d_h,
    agg_o, eg_o, kg_o, vg_o,
    ids_s, lvl_s, off_s, bias_s, q_v, lat_v, fld, wem, vem, wk, wv, wo, lsem,
    x_buf, x_ss, x_rs,
    g_snd, g_buf, g_ss, g_rs,
    ml_buf, ml_ss, ml_rs,
    r_buf, r_ss, r_rs,
    c_snd, c_buf, c_ss, c_rs,
    a_snd, a_buf, a_ss, a_rs,
    kb, kr1, kr2, kr3, ks1, ks2, kfin,
    vb, vr1, vr2, vr3, vs1, vs2, vfin,
    egb, re1, re2, e1, fine,
    k_ss, k_rs, v_ss, v_rs, e_ss, e_rs,
    wa, wat, wot, wek, wev, wekt, wevt, ff, fb, bi, ss, sn, ga, gc, at, ca, cb, eb, fg, ctxt,
):
    i, j = lax.axis_index("var"), lax.axis_index("patch")
    z, xh = i // 2, i % 2
    y, c = j // 2, j % 2
    w_me = z * 4 + y
    var_peers = [((z + a) % 4) * 2 + (xh + b) % 2 for a, b in VAR]
    patch_peers = [((y + a) % 4) * 2 + (c + b) % 2 for a, b in PATCH]
    square_peers = [((z + a) % 4, (y + b) % 4) for a, b in SQUARE]

    pending = []

    class Tr:
        def __init__(self, cp):
            self.cp = cp

        def start(self):
            self.cp.start()
            pending.append(self)

        def wait(self):
            self.cp.wait()
            pending.remove(self)

    def remote(src, dst, ssem, rsem, **dev):
        return Tr(pltpu.make_async_remote_copy(
            src_ref=src,
            dst_ref=dst,
            send_sem=ssem,
            recv_sem=rsem,
            device_id=dev,
            device_id_type=pl.DeviceIdType.MESH,
        ))

    local = [
        Tr(pltpu.make_async_copy(src, dst, lsem.at[n]))
        for n, (src, dst) in enumerate(
            [
                (fields_h, fld),
                (we_h, wem),
                (ve_h, vem.at[pl.ds(0, 240)]),
                (wk_h, wk),
                (wv_h, wv),
                (wo_h, wo),
                (d_h, x_buf.at[i]),
                (ids_h, ids_s),
                (lvl_h, lvl_s),
                (off_h, off_s),
                (bias_h, bias_s),
                (q_h, q_v),
                (lat_h, lat_v),
            ]
        )
    ]
    for cp in local:
        cp.start()

    barrier = pltpu.get_barrier_semaphore()
    peers = [dict(var=a * 2 + xh, patch=b * 2 + c) for (a, b), (d, e) in zip(square_peers, SQUARE) if d and e]
    peers += [dict(var=n) for n in var_peers] + [dict(patch=n) for n in patch_peers]
    for dev in peers:
        pl.semaphore_signal(barrier, inc=1, device_id=dev, device_id_type=pl.DeviceIdType.MESH)

    for n in range(7, 13):
        local[n].wait()
    def bias_step(v, _):
        lvl = lvl_s[ids_s[i * NV + v]]
        slot = v + v // VL
        for h in range(H):
            bi[h, pl.ds(slot, 1), :] = jnp.full((1, NP), bias_s[h, lvl], f32)
        return 0

    lax.fori_loop(0, NV, bias_step, 0)

    local[0].wait()
    lane_col = iota((8, NP), 1) >> 4
    own = lane_col == iota((8, NP), 0)
    pick = ((iota((PIX, NP), 1) & 15) == iota((PIX, NP), 0)).astype(bf16)
    for g in range(2):
        parts = []
        for v in range(VL):
            row = fld[g * VL + v].astype(f32)
            for b in range(8):
                for r in range(2):
                    piece = jnp.broadcast_to(row[r : r + 1, b * 128 : (b + 1) * 128], (8, 128))
                    parts.append(jnp.where(own, piece, 0.0))
        spread = jnp.concatenate(parts, axis=0).astype(bf16)
        ft = dot(pick, spread, NT)
        for v in range(VL):
            ff[g, v * PIX : (v + 1) * PIX, :] = ft[:, v * NP : (v + 1) * NP]
        ff[g, VL * PIX :, :] = jnp.where(iota((16, NP), 0) < VL, 1.0, 0.0)
        fb[g] = ff[g].astype(bf16)

    pl.semaphore_wait(barrier, len(peers))
    xs = [remote(d_h, x_buf.at[i], x_ss.at[n], x_rs.at[n], var=peer) for n, peer in enumerate(var_peers)]
    for cp in xs:
        cp.start()

    local[1].wait()

    def gather_step(v, _):
        g = v // VL
        row = pl.multiple_of(g * GR + (v - g * VL) * PIX, PIX)
        wa[pl.ds(row, PIX), :] = wem[ids_s[i * NV + v]]
        return 0

    lax.fori_loop(0, NV, gather_step, 0)
    vem[240:, :] = jnp.zeros((16, D), bf16)
    local[2].wait()
    for g in range(2):
        want = jnp.full((16, 256), -1, i32)
        for v in range(VL):
            want = jnp.where(iota((16, 256), 0) == v, ids_s[i * NV + g * VL + v], want)
        hot = jnp.where(want == iota((16, 256), 1), 1.0, 0.0).astype(bf16)
        wa[g * GR + VL * PIX : (g + 1) * GR, :] = dot(hot, vem[...]).astype(bf16)
    local[3].wait()
    local[4].wait()
    local[5].wait()
    wot[...] = wo[...].T
    wek[...] = dot(wa[...], wk[...]).astype(bf16)
    wev[...] = dot(wa[...], wv[...]).astype(bf16)
    for g in range(2):
        wekt[g] = wek[g * GR : (g + 1) * GR, :].T

    spread_q = jnp.where((iota((DH, D), 1) & 63) == iota((DH, D), 0), 1.0, 0.0)
    qall = jnp.dot(q_v[...], spread_q, precision=lax.Precision.HIGHEST, preferred_element_type=f32)
    qblk = jnp.where((iota((H, D), 1) >> 6) == iota((H, D), 0), qall, 0.0)
    qrow = jnp.sum(qblk, axis=0, keepdims=True)
    wq = dot(jnp.concatenate(split(qblk), axis=0), wk[...], NT)
    wq = wq[:H] + wq[H:]
    aq = dot(jnp.concatenate(split(wq), axis=0), wa[...], NT)
    aq = aq[:H] + aq[H:]
    lane_var = var_of(iota((16, GR), 1))
    member = lane_var == iota((16, GR), 0)
    sums = jnp.where(member, 1.0, 0.0).astype(bf16)
    for g in range(2):
        rows = [
            jnp.where(member, jnp.broadcast_to(aq[h : h + 1, g * GR : (g + 1) * GR], (16, GR)), 0.0)
            for h in range(H)
        ]
        hi, lo = split(jnp.concatenate(rows, axis=0))
        got = dot(hi, fb[g]) + dot(lo, fb[g])
        for h in range(H):
            sn[h, g * 16 : (g + 1) * 16, :] = got[h * 16 : (h + 1) * 16]

    heads = jnp.where((iota((16, D), 1) >> 6) == iota((16, D), 0), 1.0, 0.0).astype(bf16)
    tile_row = iota((16, NP), 0)
    def square_sums(g):
        ones = ff[g, VL * PIX :, :]
        for t in range(8):
            cols = []
            for v in (2 * t, 2 * t + 1):
                top = []
                if v < VL:
                    if v > 0:
                        top.append(jnp.zeros((v * PIX, NP), bf16))
                    top.append(fb[g, v * PIX : (v + 1) * PIX, :])
                    if v < VL - 1:
                        top.append(jnp.zeros(((VL - 1 - v) * PIX, NP), bf16))
                else:
                    top.append(jnp.zeros((VL * PIX, NP), bf16))
                top.append(jnp.where(tile_row == v, ones, 0.0).astype(bf16))
                cols.append(jnp.concatenate(top, axis=0))
            keys = dot(wekt[g], jnp.concatenate(cols, axis=1))
            sq = dot(heads, (keys * keys).astype(bf16))
            ss[:, g * 16 + 2 * t, :] = sq[:H, :NP]
            ss[:, g * 16 + 2 * t + 1, :] = sq[:H, NP:]


    square_sums(0)

    local[6].wait()
    for cp in xs:
        cp.wait()
    gx = dot(x_buf[...].reshape(NP, D), wot[...]).astype(bf16)
    o = iota((NP, NP), 0)
    src = ((o >> 1) & 7) * 16 + (o >> 4) * 2 + (o & 1)
    perm = jnp.where(src == iota((NP, NP), 1), 1.0, 0.0).astype(bf16)
    gs_rows = dot(perm, gx).astype(bf16)
    g_snd[...] = gs_rows.reshape(8, 16, D)
    gsends = []
    for n, peer in enumerate(patch_peers):
        gsends.append(remote(g_snd.at[peer], g_buf.at[j], g_ss.at[n], g_rs.at[n], patch=peer))
    for cp in gsends:
        cp.start()
    g_buf[j] = g_snd[j]

    square_sums(1)
    scale = DH**-0.5
    slot = iota((H, 32, NP), 1)
    real = (slot & 15) < VL
    inv = lax.rsqrt(ss[...] * (1.0 / DH) + 1e-6)
    s0 = scale * inv * sn[...]
    s = jnp.where(real, s0 + bi[...], -1e30)
    m = jnp.max(s, axis=1, keepdims=True)
    e = jnp.where(real, jnp.exp(s - m), 0.0)
    at[...] = e
    ml_buf[i, 0] = m[:, 0, :]
    ml_buf[i, 1] = jnp.sum(e, axis=1)
    mls = [
        remote(ml_buf.at[i], ml_buf.at[i], ml_ss.at[n], ml_rs.at[n], var=peer)
        for n, peer in enumerate(var_peers)
    ]
    for cp in mls:
        cp.start()
    sn[...] = s0
    ss[...] = inv

    for cp in gsends:
        cp.wait()
    o = iota((NP, NP), 0)
    src = (o & 7) * 16 + (o >> 4) * 2 + ((o >> 3) & 1)
    perm = jnp.where(src == iota((NP, NP), 1), 1.0, 0.0).astype(bf16)
    gcf = dot(perm, g_buf[...].reshape(NP, D))
    gc[...] = gcf.astype(bf16)
    gct = gcf.T
    top_half = iota((NP, NP), 0) < DH
    for pair in range(4):
        piece = gct[pair * 128 : (pair + 1) * 128]
        blocks = jnp.concatenate(
            [jnp.where(top_half, piece, 0.0), jnp.where(top_half, 0.0, piece)], axis=1
        ).astype(bf16)
        for g in range(2):
            prod = dot(wev[g * GR : (g + 1) * GR, pair * 128 : (pair + 1) * 128], blocks)
            fg_rows = ff[g]
            hi, lo = split(prod * jnp.concatenate([fg_rows, fg_rows], axis=1))
            got = dot(sums, hi) + dot(sums, lo)
            ga[2 * pair, g * 16 : (g + 1) * 16, :] = got[:, :NP]
            ga[2 * pair + 1, g * 16 : (g + 1) * 16, :] = got[:, NP:]
    r_buf[i] = jnp.sum(at[...] * ga[...], axis=1)
    rss = [
        remote(r_buf.at[i], r_buf.at[i], r_ss.at[n], r_rs.at[n], var=peer)
        for n, peer in enumerate(var_peers)
    ]
    for cp in rss:
        cp.start()
    wat[...] = wa[...].T
    for g in range(2):
        wevt[g] = wev[g * GR : (g + 1) * GR, :].T
    for cp in mls:
        cp.wait()
    mall = ml_buf[0, 0]
    for n in range(1, 8):
        mall = jnp.maximum(mall, ml_buf[n, 0])
    lall = jnp.zeros((H, NP), f32)
    for n in range(8):
        lall = lall + jnp.exp(ml_buf[n, 0] - mall) * ml_buf[n, 1]
    mine = jnp.exp(ml_buf[i, 0] - mall) / lall
    at[...] = at[...] * mine[:, None, :]

    def times_fields(ref, h, g):
        x = ref[h, g * 16 : (g + 1) * 16, :]
        parts = [jnp.broadcast_to(x[v : v + 1], (PIX, NP)) for v in range(VL)] + [x]
        return (jnp.concatenate(parts, axis=0) * ff[g]).astype(bf16)

    def put(buf, x):
        buf[:D, :] = x[:, : D // 2]
        buf[D:, :] = x[:, D // 2 :]

    sib = y * 2 + 1 - c

    def core_sum_start(buf, r1, s_sem, r_sem):
        cp = remote(buf.at[pl.ds((1 - c) * D, D)], r1, s_sem.at[0], r_sem.at[0], patch=sib)
        cp.start()
        return cp

    def core_sum_end(cp, buf, r1, s1, r2, s_sem, r_sem):
        cp.wait()
        s1[...] = (buf[pl.ds(c * D, D), :].astype(f32) + r1[...].astype(f32)).astype(bf16)
        cps = []
        for n, (a, b) in enumerate(square_peers):
            part = s1.at[pl.ds((a * 4 + b) * 32, 32)]
            cps.append(
                remote(part, r2.at[n], s_sem.at[n + 1], r_sem.at[n + 1], var=a * 2 + xh, patch=b * 2 + c)
            )
        for cp in cps:
            cp.start()
        return cps

    def zy_sum_end(cps, s1, r2, s2, r3, s_sem, r_sem):
        for cp in cps:
            cp.wait()
        tot = s1[pl.ds(w_me * 32, 32), :].astype(f32)
        for n in range(15):
            tot = tot + r2[n].astype(f32)
        s2[...] = tot.astype(bf16)
        cp = remote(s2, r3, s_sem.at[16], r_sem.at[16], var=z * 2 + 1 - xh)
        cp.start()
        return cp

    def x_sum_end(cp, s2, r3, fin, s_sem, r_sem):
        cp.wait()
        row = c * D + w_me * 32
        fin[pl.ds(row, 32), :] = (s2[...].astype(f32) + r3[...].astype(f32)).astype(bf16)
        rows = fin.at[pl.ds(row, 32)]
        cps = []
        for n, (a, b) in enumerate(square_peers):
            cps.append(
                remote(rows, rows, s_sem.at[17 + n], r_sem.at[17 + n], var=a * 2 + xh, patch=b * 2 + c)
            )
        for cp in cps:
            cp.start()
        return cps

    def gather_end(cps, fin, s_sem, r_sem):
        for cp in cps:
            cp.wait()
        half = fin.at[pl.ds(c * D, D)]
        cp = remote(half, half, s_sem.at[32], r_sem.at[32], patch=sib)
        cp.start()
        return cp

    low = iota((NP, 128), 1) < DH
    lowg = iota((GR, 128), 1) < DH
    zero = jnp.zeros((), bf16)
    for pair in range(4):
        lanes = slice(pair * 128, (pair + 1) * 128)
        piece = gc[:, lanes].astype(f32)
        gd = jnp.concatenate([jnp.where(low, piece, 0.0), jnp.where(low, 0.0, piece)], axis=0)
        gd = gd.astype(bf16)
        for g in range(2):
            pieces = []
            for n in range(2):
                x = times_fields(at, 2 * pair + n, g)
                eb[2 * pair + n, g * GR : (g + 1) * GR, :] = x
                pieces.append(x)
            fg[g * GR : (g + 1) * GR, D + pair * 128 : D + (pair + 1) * 128] = dot(
                jnp.concatenate(pieces, axis=1), gd
            ).astype(bf16)
    put(vb, dot(wat[...], fg[:, D:]).astype(bf16))
    v1 = core_sum_start(vb, vr1, v_ss, v_rs)


    for cp in rss:
        cp.wait()
    rall = jnp.zeros((H, NP), f32)
    for n in range(8):
        rall = rall + jnp.exp(ml_buf[n, 0] - mall) * r_buf[n]
    rall = rall / lall
    inv = ss[...]
    gs = at[...] * (ga[...] - rall[:, None, :])
    ca[...] = scale * inv * gs
    cb[...] = (-1.0 / DH) * inv * inv * gs * sn[...]

    same = var_of(iota((GR, GR), 0)) == var_of(iota((GR, GR), 1))
    for pair in range(4):
        lanes = slice(pair * 128, (pair + 1) * 128)
        qp = jnp.broadcast_to(qrow[:, lanes], (NP, 128))
        qd = jnp.concatenate([jnp.where(low, qp, 0.0), jnp.where(low, 0.0, qp)], axis=0).astype(bf16)
        for g in range(2):
            wp = wek[g * GR : (g + 1) * GR, lanes].astype(f32)
            wd = jnp.concatenate([jnp.where(lowg, wp, 0.0), jnp.where(lowg, 0.0, wp)], axis=0)
            wd = wd.astype(bf16)
            af, ms = [], []
            for n in range(2):
                af.append(times_fields(ca, 2 * pair + n, g))
                mm = dot(times_fields(cb, 2 * pair + n, g), fb[g], NT)
                ms.append(jnp.where(same, mm, 0.0).astype(bf16))
            total = dot(jnp.concatenate(af, axis=1), qd) + dot(jnp.concatenate(ms, axis=1), wd)
            fg[g * GR : (g + 1) * GR, lanes] = total.astype(bf16)
    put(kb, dot(wat[...], fg[:, :D]).astype(bf16))
    k1 = core_sum_start(kb, kr1, k_ss, k_rs)
    v2 = core_sum_end(v1, vb, vr1, vs1, vr2, v_ss, v_rs)
    k2 = core_sum_end(k1, kb, kr1, ks1, kr2, k_ss, k_rs)
    def embed_grad(g):
        rows = pl.ds(pl.multiple_of(g * GR, GR), GR)
        egb[rows, :] = (dot(fg[rows, :D], wk[...], NT) + dot(fg[rows, D:], wv[...], NT)).astype(bf16)

    embed_grad(1 - c)
    ex1 = remote(egb.at[pl.ds((1 - c) * GR, GR)], re1, e_ss.at[0], e_rs.at[0], patch=sib)
    ex1.start()
    embed_grad(c)
    ex1.wait()
    e1[...] = (egb[pl.ds(c * GR, GR), :].astype(f32) + re1[...].astype(f32)).astype(bf16)
    ex2 = []
    for t in range(1, 4):
        peer = (y + t) % 4
        ex2.append(
            remote(e1.at[pl.ds(peer * 64, 64)], re2.at[t - 1], e_ss.at[t], e_rs.at[t], patch=peer * 2 + c)
        )
    for cp in ex2:
        cp.start()

    for h in range(H):
        acc = dot(wevt[0, h * DH : (h + 1) * DH, :], eb[h, :GR, :])
        acc = acc + dot(wevt[1, h * DH : (h + 1) * DH, :], eb[h, GR:, :])
        ctxt[h * DH : (h + 1) * DH, :] = acc
    c_snd[...] = ctxt[...].T.astype(bf16).reshape(8, 16, D)
    cs = []
    for n, peer in enumerate(var_peers):
        cs.append(remote(c_snd.at[peer], c_buf.at[i], c_ss.at[n], c_rs.at[n], var=peer))
    for cp in cs:
        cp.start()
    c_buf[i] = c_snd[i]

    v3 = zy_sum_end(v2, vs1, vr2, vs2, vr3, v_ss, v_rs)
    k3 = zy_sum_end(k2, ks1, kr2, ks2, kr3, k_ss, k_rs)
    v4 = x_sum_end(v3, vs2, vr3, vfin, v_ss, v_rs)
    for cp in ex2:
        cp.wait()
    tot = e1[pl.ds(y * 64, 64), :].astype(f32)
    for n in range(3):
        tot = tot + re2[n].astype(f32)
    erow = c * GR + y * 64
    fine[pl.ds(erow, 64), :] = tot.astype(bf16)
    ex3 = []
    for t in range(1, 4):
        peer = (y + t) % 4
        own_rows = fine.at[pl.ds(erow, 64)]
        ex3.append(remote(own_rows, own_rows, e_ss.at[3 + t], e_rs.at[3 + t], patch=peer * 2 + c))
    for cp in ex3:
        cp.start()
    k4 = x_sum_end(k3, ks2, kr3, kfin, k_ss, k_rs)
    for cp in cs:
        cp.wait()
    cx = c_buf[0].astype(f32)
    for n in range(1, 8):
        cx = cx + c_buf[n].astype(f32)
    row = off_s[0] + 2 * j + (iota((16, 180), 0) >> 3)
    hot = jnp.where(row == iota((16, 180), 1), 1.0, 0.0).astype(bf16)
    agg = (dot(cx.astype(bf16), wo[...]) + dot(hot, lat_v[...])).astype(bf16)
    dst = iota((NP, 16), 0)
    r = (dst & 15) - 2 * j
    take = ((r >= 0) & (r < 2)) & (iota((NP, 16), 1) == r * 8 + (dst >> 4))
    a_snd[...] = dot(jnp.where(take, 1.0, 0.0).astype(bf16), agg).astype(bf16).reshape(8, 16, D)
    sends = []
    for n, peer in enumerate(patch_peers):
        sends.append(remote(a_snd.at[peer], a_buf.at[j], a_ss.at[n], a_rs.at[n], patch=peer))
    for cp in sends:
        cp.start()
    a_buf[j] = a_snd[j]

    for cp in ex3:
        cp.wait()
    half = fine.at[pl.ds(c * GR, GR)]
    ex4 = remote(half, half, e_ss.at[7], e_rs.at[7], patch=sib)
    ex4.start()

    for cp in sends:
        cp.wait()
    acc = a_buf[0].astype(f32)
    for n in range(1, 8):
        acc = acc + a_buf[n].astype(f32)
    a_snd[0] = acc.astype(bf16)
    outs = [pltpu.make_async_copy(a_snd.at[0], agg_o, lsem.at[13])]
    outs[0].start()
    def store(ref, out, side, rows, n):
        part = pl.ds(side * rows, rows)
        outs.append(pltpu.make_async_copy(ref.at[part], out.at[part], lsem.at[n]))
        outs[-1].start()

    store(fine, eg_o, c, GR, 14)
    ex4.wait()
    store(fine, eg_o, 1 - c, GR, 15)
    v5 = gather_end(v4, vfin, v_ss, v_rs)
    store(vfin, vg_o, c, D, 16)
    k5 = gather_end(k4, kfin, k_ss, k_rs)
    store(kfin, kg_o, c, D, 17)
    v5.wait()
    store(vfin, vg_o, 1 - c, D, 18)
    k5.wait()
    store(kfin, kg_o, 1 - c, D, 19)
    for cp in outs:
        cp.wait()


def cast_kernel(agg_h, eg_h, kg_h, vg_h, agg_o, emb_o, var_o, kg_o, vg_o, agg, eg, kg, vg, emb, var, kgf, vgf, sem):
    def copy(n, src, dst):
        cp = pltpu.make_async_copy(src, dst, sem.at[n])
        cp.start()
        return cp

    first = [copy(0, vg_h, vg), copy(1, kg_h, kg), copy(2, eg_h, eg), copy(3, agg_h, agg)]
    outs = []
    for n, (src, full, dst) in enumerate(((vg, vgf, vg_o), (kg, kgf, kg_o))):
        first[n].wait()
        full[:, : D // 2] = src[:D].astype(f32)
        full[:, D // 2 :] = src[D:].astype(f32)
        outs.append(copy(4 + n, full, dst))
    first[2].wait()
    for g in range(2):
        emb[g * VL : (g + 1) * VL] = eg[g * GR : g * GR + VL * PIX].astype(f32).reshape(VL, PIX, D)
        var[g * VL : (g + 1) * VL] = eg[g * GR + VL * PIX : (g + 1) * GR].astype(f32)[:VL]
    outs += [copy(6, emb, emb_o), copy(7, var, var_o)]
    first[3].wait()
    outs.append(copy(8, agg, agg_o))
    for cp in outs:
        cp.wait()


def local(fields, var_ids, level_of, window_offset, w_embed, var_emb, w_key, w_value, w_out,
          latent_query, bias_table, lat_emb, d_aggregated):
    hbm = pl.BlockSpec(memory_space=pltpu.HBM)
    dma = pltpu.SemaphoreType.DMA

    def v(*shape, dtype=bf16):
        return pltpu.VMEM(shape, dtype)

    scratch = [
        pltpu.SMEM((240,), i32), pltpu.SMEM((240,), i32), pltpu.SMEM((1,), i32), pltpu.SMEM((H, 38), f32),
        v(H, DH, dtype=f32), v(180, D), v(NV, 2, 1024), v(240, PIX, D), v(256, D), v(D, D), v(D, D), v(D, D), dma((20,)),
        v(8, 16, D), dma((7,)), dma((7,)),
        v(8, 16, D), v(8, 16, D), dma((7,)), dma((7,)),
        v(8, 2, H, NP, dtype=f32), dma((7,)), dma((7,)),
        v(8, H, NP, dtype=f32), dma((7,)), dma((7,)),
        v(8, 16, D), v(8, 16, D), dma((7,)), dma((7,)),
        v(8, 16, D), v(8, 16, D), dma((7,)), dma((7,)),
        v(2 * D, D // 2), v(D, D // 2), v(15, 32, D // 2), v(32, D // 2), v(D, D // 2), v(32, D // 2), v(2 * D, D // 2),
        v(2 * D, D // 2), v(D, D // 2), v(15, 32, D // 2), v(32, D // 2), v(D, D // 2), v(32, D // 2), v(2 * D, D // 2),
        v(D, D), v(GR, D), v(3, 64, D), v(GR, D), v(D, D),
        dma((33,)), dma((33,)), dma((33,)), dma((33,)), dma((8,)), dma((8,)),
        v(D, D), v(D, D), v(D, D), v(D, D), v(D, D), v(2, D, GR), v(2, D, GR),
        v(2, GR, NP, dtype=f32), v(2, GR, NP),
    ]
    scratch += [v(H, 32, NP, dtype=f32)] * 4 + [v(NP, D)] + [v(H, 32, NP, dtype=f32)] * 3
    scratch += [v(H, D, NP), v(D, 2 * D), v(D, NP, dtype=f32)]
    agg, eg, kg, vg = pl.pallas_call(
        kernel,
        out_shape=[
            jax.ShapeDtypeStruct((16, D), bf16),
            jax.ShapeDtypeStruct((D, D), bf16),
            jax.ShapeDtypeStruct((2 * D, D // 2), bf16),
            jax.ShapeDtypeStruct((2 * D, D // 2), bf16),
        ],
        in_specs=[hbm] * 13,
        out_specs=[hbm] * 4,
        scratch_shapes=scratch,
        compiler_params=pltpu.CompilerParams(
            collective_id=0, has_side_effects=True, vmem_limit_bytes=62 * 1024 * 1024
        ),
    )(
        var_ids, level_of, window_offset, bias_table.T,
        fields, w_embed, var_emb, w_key, w_value, w_out, latent_query, lat_emb,
        d_aggregated.reshape(16, D),
    )
    agg, embed, var, key_grad, value_grad = pl.pallas_call(
        cast_kernel,
        out_shape=[
            jax.ShapeDtypeStruct((16, D), bf16),
            jax.ShapeDtypeStruct((NV, PIX, D), f32),
            jax.ShapeDtypeStruct((NV, D), f32),
            jax.ShapeDtypeStruct((D, D), f32),
            jax.ShapeDtypeStruct((D, D), f32),
        ],
        in_specs=[hbm] * 4,
        out_specs=[hbm] * 5,
        scratch_shapes=[
            v(16, D), v(D, D), v(2 * D, D // 2), v(2 * D, D // 2),
            v(NV, PIX, D, dtype=f32), v(NV, D, dtype=f32), v(D, D, dtype=f32), v(D, D, dtype=f32),
            dma((9,)),
        ],
        compiler_params=pltpu.CompilerParams(vmem_limit_bytes=62 * 1024 * 1024),
    )(agg, eg, kg, vg)
    return agg.reshape(16, 1, D), embed, var, key_grad, value_grad


def solution(mesh):
    split_rows = P(("win", "var"), "patch", None)
    column = P("win", ("var", "patch"), None)
    in_specs = (split_rows, P(), P(), P("win")) + (P(),) * 8 + (column,)
    out_specs = (
        column,
        P(("win", "var"), None, None),
        P(("win", "var"), None),
        P("win", None),
        P("win", None),
    )
    return jax.shard_map(local, mesh=mesh, in_specs=in_specs, out_specs=out_specs, check_vma=False)
```
